32 devices in a mesh: dp: 4 (over y, core), space: 8 (over z, x).
Axes of the slice: x: 2, y: 2, z: 4, core: 2. Of those that a mesh axis runs over, the one named last changes fastest.
Arguments:
- features: bfloat16 [4, 256, 64, 512], P('dp', 'space'), may hold values from -50 to 50
- owners: int32 [4, 256, 1], P('dp', 'space'), may hold values from 0 to 7; in each aligned block of 32 rows (0 to 31, 32 to 63, ..., all dimensions but the last counted through in order) at most 8 rows name the same one
- neighbors: int32 [4, 256, 3], P('dp', 'space'), may hold values from -1 to 254, as said below
- w_reduce: bfloat16 [512, 128], replicated, may hold values from -0.25 to 0.25
- w_spatial: bfloat16 [1152, 128], replicated, may hold values from -0.1875 to 0.1875
- w_expand: bfloat16 [128, 512], replicated, may hold values from -0.5 to 0.5
- w_short: bfloat16 [512, 512], replicated, may hold values from -0.25 to 0.25
- gains_mid: float32 [2, 128], replicated, may hold values from 0.25 to 1.75
- shifts_mid: float32 [2, 128], replicated, may hold values from -2.5 to 2.5
- gains_wide: float32 [2, 512], replicated, may hold values from 0.25 to 1.75
- shifts_wide: float32 [2, 512], replicated, may hold values from -2.5 to 2.5
- cotangent: bfloat16 [4, 512, 16, 512], P('dp', 'space'), may hold values from -6 to 6
Outputs:
- block_out: bfloat16 [4, 512, 16, 512], P('dp', 'space')
- grad_features: bfloat16 [4, 256, 64, 512], P('dp', 'space')
- grad_reduce: float32 [512, 128], P('space')
- grad_spatial: float32 [1152, 128], P('space')
- grad_expand: float32 [128, 512], P('space')
- grad_short: float32 [512, 512], P('space')
- grad_gains_mid: float32 [2, 128], P(None, 'space')
- grad_shifts_mid: float32 [2, 128], P(None, 'space')
- grad_gains_wide: float32 [2, 512], P(None, 'space')
- grad_shifts_wide: float32 [2, 512], P(None, 'space')
The draws below stay inside these ranges and needn't reach their ends.
Inputs may be any that keep to these rules, and one draw needn't show every extreme that they name: `owners`: among the 32 tiles of one block no owner is named more than 8 times. `neighbors`: entries are tile indices of the same slide or -1 for none; for tile t every index lies between t - 32 and t - 1.
All inputs are finite; a program needn't handle non-finite values.
Results may differ from the reference program's by a relative error of at most 0.02.
Values may be sent and summed in bfloat16 or wider, within the bound.
A program may use at most 64 MiB of HBM per device.

```python
import math
import jax
import jax.numpy as jnp
import numpy as np
from jax import lax

C_IN = 512
C_MID = 128
GROUPS = 32
SIDE = 8
TILE_DEV = 32
BLOCKS = 8
SLIDES = 4
TILES = 256
CAP = 8
SLOTS = 512


def draw_features(key, part):
    folded = jax.random.fold_in(key, 11)
    subkeys = jax.random.split(folded, 3)
    tile_place = jnp.arange(TILES, dtype=jnp.float32) / TILES
    tile_scale = jnp.exp(math.log(3.0) * tile_place[None, :] + jax.random.uniform(subkeys[0], (SLIDES, TILES), jnp.float32, 0.0, math.log(3.3)))
    chan_scale = jnp.exp(jax.random.uniform(subkeys[1], (C_IN,), jnp.float32, 0.0, math.log(10.0)))
    noise_draw = jnp.clip(jax.random.normal(subkeys[2], (SLIDES, TILES, SIDE * SIDE, C_IN), jnp.float32), -4.0, 4.0)
    values = noise_draw * tile_scale[:, :, None, None] * chan_scale / 8.0
    return values.astype(jnp.bfloat16)


def draw_neighbors(key, part):
    folded = jax.random.fold_in(key, 23)
    subkeys = jax.random.split(folded, 2)
    tile_ids = jnp.arange(TILES, dtype=jnp.int32)[None, :]
    step_up = jax.random.randint(subkeys[0], (SLIDES, TILES), 2, TILE_DEV, dtype=jnp.int32)
    step_up = jnp.where(tile_ids % 8 == 3, TILE_DEV - 1, step_up)
    upward = tile_ids - step_up
    leftward = jnp.broadcast_to(tile_ids - 1, (SLIDES, TILES))
    corner = upward - 1
    stacked = jnp.stack([upward, leftward, corner], axis=-1)
    kept_mask = jax.random.randint(subkeys[1], (SLIDES, TILES, 3), 0, 8, dtype=jnp.int32) != 0
    return jnp.where(kept_mask & (stacked >= 0), stacked, -1).astype(jnp.int32)


def draw_cotangent(key, part):
    folded = jax.random.fold_in(key, 37)
    subkeys = jax.random.split(folded, 4)
    quarter = SIDE // 2 * (SIDE // 2)
    full_shape = (SLIDES, SLOTS, quarter, C_IN)
    slide_sign = jnp.where(jax.random.uniform(subkeys[0], (SLIDES, 1, 1, 1), jnp.float32) < 0.5, -1.0, 1.0)
    channel_part = jnp.clip(jax.random.normal(subkeys[2], (SLIDES, 1, 1, C_IN), jnp.float32), -2.0, 2.0)
    common = slide_sign * jax.random.uniform(subkeys[1], (SLIDES, 1, 1, 1), jnp.float32, 0.5, 0.8)
    noise_draw = jnp.clip(jax.random.normal(subkeys[3], full_shape, jnp.float32), -4.0, 4.0)
    values = noise_draw + common + 0.6 * channel_part
    return jnp.clip(values, -6.0, 6.0).astype(jnp.bfloat16)


def shared_out(key, own, number, rows, amount, top, reach, lean):
    sequence = jax.random.permutation(key, amount)
    packed, ordinary = shares(amount, rows * top, reach, lean, True), shares(amount, rows * top, reach, lean, False)
    places = jnp.arange(amount)

    def named(tallies, rotation):
        used = int((tallies > 0).sum())
        fixed = max(1, used // 4)
        moved = fixed + (places - fixed + rotation * (used - fixed)) % max(1, amount - fixed)
        return jnp.zeros((amount,), jnp.int32).at[sequence[jnp.where(places < fixed, places, moved)]].set(jnp.asarray(tallies, jnp.int32))

    tallies = jnp.where(number % 4 == 0, named(packed, number // 4), named(ordinary, number - number // 4 - 1))
    mixed = jax.random.permutation(jax.random.fold_in(own, 3), amount)
    giver, taker = mixed[0:amount // 2 * 2:2], mixed[1:amount // 2 * 2:2]
    room = jnp.minimum(tallies[giver] - 1, reach - tallies[taker]) // 2
    room = jnp.where((giver == sequence[0]) | (taker == sequence[0]) | (tallies[taker] == 0), 0, jnp.maximum(room, 0))
    moved = jax.random.randint(jax.random.fold_in(own, 4), (amount // 2,), 0, 1 << 20) % (room + 1)
    tallies = tallies.at[giver].add(-moved).at[taker].add(moved)
    labels = jnp.searchsorted(jnp.cumsum(tallies), jnp.arange(rows * top), side="right").astype(jnp.int32)
    grid = labels.reshape(top, rows).T
    grid = grid[jax.random.permutation(jax.random.fold_in(own, 1), rows)]
    rotation = jax.random.randint(jax.random.fold_in(own, 2), (rows, 1), 0, top)
    return jnp.take_along_axis(grid, (jnp.arange(top)[None, :] + rotation) % top, axis=1)


def shares(amount, total, reach, skew, full):
    loads = [(1 << 20) // math.isqrt(rank ** skew) + 1 for rank in range(1, amount + 1)]
    largest = reach if full else min(reach, max(-(-total // amount), total * loads[0] // sum(loads)))
    least = 1 if total - largest >= amount - 1 else 0
    holding, rest = [largest] + [least] * (amount - 1), total - largest - least * (amount - 1)
    while rest > 0:
        movable = [i for i in range(1, amount) if holding[i] < largest] or [i for i in range(1, amount) if holding[i] < reach]
        whole, left = sum([loads[i] for i in movable]), rest
        for i in movable:
            extra = min(reach - holding[i], max(1, left * loads[i] // whole), rest)
            holding[i] = holding[i] + extra
            rest = rest - extra
    return np.array(holding)


def scatter_about(rng, extent, deviation, most, held_as=jnp.bfloat16):
    entries = jax.random.normal(rng, extent, jnp.float32) * deviation
    return jnp.minimum(jnp.maximum(entries, -most), most).astype(held_as)


def setup_inputs(seed: int = 0) -> dict:
    key_of = jax.random.split(jax.random.key(seed), 13)
    features = draw_features(jax.random.fold_in(key_of[12], 71), 0)
    owners_keys = jax.random.split(jax.random.fold_in(key_of[1], 1), SLIDES * TILES // TILE_DEV)
    owners_turns = jax.random.permutation(jax.random.fold_in(key_of[1], 3), SLIDES * TILES // TILE_DEV)
    owners = jax.vmap(lambda own, number: shared_out(jax.random.fold_in(key_of[1], 2), own, number, TILE_DEV, BLOCKS, 1, CAP, 2))(owners_keys, owners_turns).reshape((SLIDES, TILES, 1))
    neighbors = draw_neighbors(jax.random.fold_in(key_of[12], 71), 0)
    w_reduce = scatter_about(key_of[3], (C_IN, C_MID), C_IN ** -0.5, 0.25)
    w_spatial = scatter_about(key_of[4], (9 * C_MID, C_MID), (9 * C_MID) ** -0.5, 0.1875)
    w_expand = scatter_about(key_of[5], (C_MID, C_IN), C_MID ** -0.5, 0.5)
    w_short = scatter_about(key_of[6], (C_IN, C_IN), C_IN ** -0.5, 0.25)
    gains_mid = jnp.clip(1.0 + 0.15 * jax.random.normal(key_of[7], (2, C_MID), jnp.float32), 0.25, 1.75)
    shifts_mid = scatter_about(key_of[8], (2, C_MID), 0.5, 2.5, jnp.float32)
    gains_wide = jnp.clip(1.0 + 0.15 * jax.random.normal(key_of[9], (2, C_IN), jnp.float32), 0.25, 1.75)
    shifts_wide = scatter_about(key_of[10], (2, C_IN), 0.5, 2.5, jnp.float32)
    cotangent = draw_cotangent(jax.random.fold_in(key_of[12], 71), 0)
    return dict(features=features, owners=owners, neighbors=neighbors, w_reduce=w_reduce, w_spatial=w_spatial, w_expand=w_expand, w_short=w_short, gains_mid=gains_mid, shifts_mid=shifts_mid, gains_wide=gains_wide, shifts_wide=shifts_wide, cotangent=cotangent)


EPS = 1e-05

def smooth(values):
    return values * jax.nn.sigmoid(values)

def smooth_slope(values):
    sig = jax.nn.sigmoid(values)
    return sig * (1.0 + values * (1.0 - sig))

def group_total(per_channel):
    width = per_channel.shape[-1]
    grouped = per_channel.reshape(per_channel.shape[:-1] + (GROUPS, width // GROUPS))
    return jnp.repeat(lax.optimization_barrier(jnp.sum(grouped, axis=-1)), width // GROUPS, axis=-1)

def moments(conv_out):
    values = conv_out.astype(jnp.float32)
    return jnp.stack([lax.optimization_barrier(jnp.sum(values, axis=0)), lax.optimization_barrier(jnp.sum(values * values, axis=0))])

def grad_moments(upstream, normed):
    return jnp.stack([lax.optimization_barrier(jnp.sum(upstream, axis=0)), lax.optimization_barrier(jnp.sum(upstream * normed, axis=0))])

def norm_forward(conv_out, totals, members, gain_row, shift_row):
    center = group_total(totals[0]) / members
    spread = group_total(totals[1]) / members - center * center
    inv_spread = lax.rsqrt(spread + EPS)
    normed = (conv_out.astype(jnp.float32) - center) * inv_spread
    return (normed, normed * gain_row + shift_row, center, inv_spread)

def norm_backward(upstream, normed, inv_spread, gain_row, totals, members):
    first = group_total(gain_row * totals[0]) / members
    second = group_total(gain_row * totals[1]) / members
    return inv_spread * (gain_row * upstream - first - normed * second)

def slide_pass(tile_feats, owner_of, links, w_reduce, w_spatial, w_expand, w_short, gains_mid, shifts_mid, gains_wide, shifts_wide, cot_slide):
    half = SIDE // 2
    quarter = half * half
    members_in = TILES * SIDE * SIDE * (C_MID // GROUPS)
    members_mid = TILES * quarter * (C_MID // GROUPS)
    members_wide = TILES * quarter * (C_IN // GROUPS)
    flat_in = tile_feats.reshape(TILES * SIDE * SIDE, C_IN)
    conv_one = jnp.dot(flat_in, w_reduce, preferred_element_type=jnp.float32).astype(jnp.bfloat16)
    normed_one, pre_one, center_one, scale_one = norm_forward(conv_one, moments(conv_one), members_in, gains_mid[0], shifts_mid[0])
    act_one = smooth(pre_one).astype(jnp.bfloat16)
    safe_links = jnp.where(links < 0, TILES, links).astype(jnp.int32)
    grid_act = act_one.reshape(TILES, SIDE, SIDE, C_MID)
    blank = jnp.zeros((1, SIDE, C_MID), jnp.bfloat16)
    row_ext = jnp.concatenate([grid_act[:, SIDE - 1], blank], axis=0)
    col_ext = jnp.concatenate([grid_act[:, :, SIDE - 1], blank], axis=0)
    top_row = row_ext[safe_links[:, 0]]
    left_col = col_ext[safe_links[:, 1]]
    corner_cell = row_ext[safe_links[:, 2], SIDE - 1]
    first_line = jnp.concatenate([corner_cell[:, None], top_row], axis=1)
    lower_rows = jnp.concatenate([left_col[:, :, None], grid_act], axis=2)
    padded = jnp.concatenate([first_line[:, None], lower_rows], axis=1)
    columns = jnp.concatenate([padded[:, offset_row:offset_row + SIDE - 1:2, offset_col:offset_col + SIDE - 1:2] for offset_row in range(3) for offset_col in range(3)], axis=-1).reshape(TILES * quarter, 9 * C_MID)
    conv_two = jnp.dot(columns, w_spatial, preferred_element_type=jnp.float32).astype(jnp.bfloat16)
    normed_two, pre_two, center_two, scale_two = norm_forward(conv_two, moments(conv_two), members_mid, gains_mid[1], shifts_mid[1])
    act_two = smooth(pre_two).astype(jnp.bfloat16)
    conv_three = jnp.dot(act_two, w_expand, preferred_element_type=jnp.float32).astype(jnp.bfloat16)
    sub_in = tile_feats.reshape(TILES, SIDE, SIDE, C_IN)[:, ::2, ::2].reshape(TILES * quarter, C_IN)
    conv_short = jnp.dot(sub_in, w_short, preferred_element_type=jnp.float32).astype(jnp.bfloat16)
    normed_three, pre_three, center_three, scale_three = norm_forward(conv_three, moments(conv_three), members_wide, gains_wide[0], shifts_wide[0])
    normed_short, pre_short, center_short, scale_short = norm_forward(conv_short, moments(conv_short), members_wide, gains_wide[1], shifts_wide[1])
    summed = pre_three + pre_short
    result = smooth(summed).astype(jnp.bfloat16)
    owner_hits = (owner_of[:, None] == jnp.arange(BLOCKS, dtype=jnp.int32)[None, :]).astype(jnp.int32).reshape(BLOCKS, TILE_DEV, BLOCKS)
    before = jnp.cumsum(owner_hits, axis=1) - owner_hits
    rank_in = lax.optimization_barrier(jnp.sum(before * owner_hits, axis=2)).reshape(TILES).astype(jnp.int32)
    source = jnp.arange(TILES, dtype=jnp.int32) // TILE_DEV
    slot_of = (owner_of * (BLOCKS * CAP) + source * CAP + rank_in).astype(jnp.int32)
    out_slide = jnp.zeros((SLOTS, quarter, C_IN), jnp.bfloat16).at[slot_of].set(result.reshape(TILES, quarter, C_IN))
    picked = cot_slide[slot_of].reshape(TILES * quarter, C_IN).astype(jnp.float32)
    upstream = picked * smooth_slope(summed)
    totals_three = grad_moments(upstream, normed_three)
    totals_short = grad_moments(upstream, normed_short)
    dconv_three = norm_backward(upstream, normed_three, scale_three, gains_wide[0], totals_three, members_wide).astype(jnp.bfloat16)
    dconv_short = norm_backward(upstream, normed_short, scale_short, gains_wide[1], totals_short, members_wide).astype(jnp.bfloat16)
    grad_expand_part = jnp.dot(act_two.T, dconv_three, preferred_element_type=jnp.float32)
    grad_short_part = jnp.dot(sub_in.T, dconv_short, preferred_element_type=jnp.float32)
    back_two = jnp.dot(dconv_three, w_expand.T, preferred_element_type=jnp.float32)
    back_two = back_two * smooth_slope(pre_two)
    totals_two = grad_moments(back_two, normed_two)
    dconv_two = norm_backward(back_two, normed_two, scale_two, gains_mid[1], totals_two, members_mid).astype(jnp.bfloat16)
    grad_spatial_part = jnp.dot(columns.T, dconv_two, preferred_element_type=jnp.float32)
    back_cols = jnp.dot(dconv_two, w_spatial.T, preferred_element_type=jnp.float32).reshape(TILES, half, half, 9, C_MID)
    back_pad = jnp.zeros((TILES, SIDE + 1, SIDE + 1, C_MID), jnp.float32)
    for offset_row in range(3):
        for offset_col in range(3):
            back_pad = back_pad.at[:, offset_row:offset_row + SIDE - 1:2, offset_col:offset_col + SIDE - 1:2].add(back_cols[:, :, :, 3 * offset_row + offset_col])
    rows_acc = jnp.zeros((TILES + 1, SIDE, C_MID), jnp.float32).at[safe_links[:, 0]].add(back_pad[:, 0, 1:])
    rows_acc = rows_acc.at[safe_links[:, 2], SIDE - 1].add(back_pad[:, 0, 0])
    cols_acc = jnp.zeros((TILES + 1, SIDE, C_MID), jnp.float32).at[safe_links[:, 1]].add(back_pad[:, 1:, 0])
    inner = back_pad[:, 1:, 1:]
    inner = inner.at[:, SIDE - 1].add(rows_acc[:TILES]).at[:, :, SIDE - 1].add(cols_acc[:TILES])
    back_one = (inner * smooth_slope(pre_one).reshape(TILES, SIDE, SIDE, C_MID)).reshape(TILES * SIDE * SIDE, C_MID)
    totals_one = grad_moments(back_one, normed_one)
    dconv_one = norm_backward(back_one, normed_one, scale_one, gains_mid[0], totals_one, members_in).astype(jnp.bfloat16)
    grad_reduce_part = jnp.dot(flat_in.T, dconv_one, preferred_element_type=jnp.float32)
    back_in = jnp.dot(dconv_one, w_reduce.T, preferred_element_type=jnp.float32).reshape(TILES, SIDE, SIDE, C_IN)
    back_short = jnp.dot(dconv_short, w_short.T, preferred_element_type=jnp.float32).reshape(TILES, half, half, C_IN)
    back_in = back_in.at[:, ::2, ::2].add(back_short)
    grad_feat = back_in.reshape(TILES, SIDE * SIDE, C_IN).astype(jnp.bfloat16)
    partials = (grad_reduce_part, grad_spatial_part, grad_expand_part, grad_short_part, jnp.stack([totals_one[1], totals_two[1]]), jnp.stack([totals_one[0], totals_two[0]]), jnp.stack([totals_three[1], totals_short[1]]), jnp.stack([totals_three[0], totals_short[0]]))
    return (out_slide, grad_feat, partials)

def reference(features, owners, neighbors, w_reduce, w_spatial, w_expand, w_short, gains_mid, shifts_mid, gains_wide, shifts_wide, cotangent):
    out_list = []
    grad_list = []
    running = None
    for slide in range(SLIDES):
        out_slide, grad_feat, partials = slide_pass(features[slide], owners[slide, :, 0], neighbors[slide], w_reduce, w_spatial, w_expand, w_short, gains_mid, shifts_mid, gains_wide, shifts_wide, cotangent[slide])
        out_list.append(out_slide)
        grad_list.append(grad_feat)
        if running is None:
            running = partials
        else:
            running = jax.tree.map(jnp.add, running, partials)
    scale_in = 1.0 / math.sqrt(SLIDES * TILES * SIDE * SIDE)
    scale_out = 1.0 / math.sqrt(SLIDES * TILES * (SIDE // 2) * (SIDE // 2))
    mid_scale = jnp.array([[scale_in], [scale_out]], jnp.float32)
    return (jnp.stack(out_list), jnp.stack(grad_list), running[0] * scale_in, running[1] * scale_out, running[2] * scale_out, running[3] * scale_out, running[4] * mid_scale, running[5] * mid_scale, running[6] * scale_out, running[7] * scale_out)
```

```python
import functools
import math

import jax
import jax.numpy as jnp
import numpy as np
from jax import lax
from jax.experimental import pallas as pl
from jax.experimental.pallas import tpu as pltpu
from jax.sharding import PartitionSpec as P

GROUPS = 32
SIDE = 8
HALF = SIDE // 2
Q = HALF * HALF
EPS = 1e-05
MESH = pl.DeviceIdType.MESH
F32 = jnp.float32
BF16 = jnp.bfloat16
STEP = 4
BLOCK = 128


def sigmoid(v):
    return 1.0 / (1.0 + jnp.exp(-v))


def smooth(v):
    return v * sigmoid(v)


def slope(v):
    s = sigmoid(v)
    return s * (1.0 + v * (1.0 - s))


def mm(a, b):
    return lax.dot_general(a, b, (((1,), (0,)), ((), ())), preferred_element_type=F32)


def mm_t(a, b):
    return lax.dot_general(a, b, (((1,), (1,)), ((), ())), preferred_element_type=F32)


def t_mm(a, b):
    return lax.dot_general(a, b, (((0,), (0,)), ((), ())), preferred_element_type=F32)


def group_sum(rows):
    width = rows.shape[-1]
    each = width // GROUPS
    a = lax.broadcasted_iota(jnp.int32, (width, width), 0) // each
    b = lax.broadcasted_iota(jnp.int32, (width, width), 1) // each
    same = jnp.where(a == b, 1.0, 0.0).astype(F32)
    return lax.dot_general(
        rows,
        same,
        (((1,), (0,)), ((), ())),
        precision=lax.Precision.HIGHEST,
        preferred_element_type=F32,
    )


def norm_of(tot, first, width, members):
    g = group_sum(tot[:, :width])
    center = g[first : first + 1] / members
    spread = g[first + 1 : first + 2] / members - center * center
    return center, lax.rsqrt(spread + EPS)


def back_of(tot, first, second, gain, width, members):
    g = group_sum(tot[:, :width] * gain)
    return g[first : first + 1] / members, g[second : second + 1] / members


def sums(v):
    return jnp.sum(v, axis=0, keepdims=True)


def onehot(index, axis, shape):
    return jnp.where(lax.broadcasted_iota(jnp.int32, shape, axis) == index, 1.0, 0.0).astype(BF16)


def block(i, size):
    return pl.ds(pl.multiple_of(i * size, size), size)


def first_kernel(feat, w_reduce, w_short, sel, conv1, sub_in, conv_short, mom):
    rows = STEP * SIDE * SIDE
    part = STEP * Q
    wide = w_short.shape[1]
    mid = w_reduce.shape[1]

    def step(g, carry):
        s1, q1, s2, q2 = carry
        x = feat[block(g, rows), :]
        c = mm(x, w_reduce[...]).astype(BF16)
        cf = c.astype(F32)
        p = mm(sel[...], c).astype(BF16)
        for k in range(4):
            conv1[k, block(g, part), :] = p[k * part : (k + 1) * part]
        sub = mm(sel[:part, :], x).astype(BF16)
        sub_in[block(g, part), :] = sub
        sh = mm(sub, w_short[...]).astype(BF16)
        conv_short[block(g, part), :] = sh
        sf = sh.astype(F32)
        return s1 + sums(cf), q1 + sums(cf * cf), s2 + sums(sf), q2 + sums(sf * sf)

    z1, z2 = jnp.zeros((1, mid), F32), jnp.zeros((1, wide), F32)
    s1, q1, s2, q2 = lax.fori_loop(0, feat.shape[0] // rows, step, (z1, z1, z2, z2))
    mom[...] = jnp.zeros_like(mom)
    mom[0:1, :mid] = s1
    mom[1:2, :mid] = q1
    mom[2:3, :] = s2
    mom[3:4, :] = q2


def act_kernel(members, conv1, tot1, gm, sm, ends, act, rim):
    mid = conv1.shape[2]
    center, inv = norm_of(tot1[...], 0, mid, members)
    for k in range(4):

        def step(i, _, k=k):
            v = (conv1[k, block(i, BLOCK), :].astype(F32) - center) * inv
            act[k, block(i, BLOCK), :] = smooth(v * gm[0:1] + sm[0:1]).astype(BF16)
            return 0

        lax.fori_loop(0, conv1.shape[1] // BLOCK, step, 0)
    count = ends.shape[0] // 2
    for k, e, lane in ((2, 0, 0), (3, 0, 1), (1, 1, 0), (3, 1, 1)):
        rim[e * count : (e + 1) * count, lane * mid : (lane + 1) * mid] = mm(
            ends[e * count : (e + 1) * count, :], act[k]
        ).astype(BF16)


def conv2_kernel(act, rim, src, w_spatial, columns, conv2, mom):
    mid = act.shape[2]
    own = act.shape[1]
    far = rim.shape[0] // 2

    def step(i, carry):
        s, q = carry
        rows = block(i, BLOCK)
        at = src[rows, :]
        top = onehot(at[:, 0:1], 1, (BLOCK, own + far))
        left = onehot(at[:, 1:2], 1, (BLOCK, own + far))
        corner = onehot(at[:, 2:3], 1, (BLOCK, own + 2 * far))

        def put(slot, v):
            columns[rows, slot * mid : (slot + 1) * mid] = v.astype(BF16)

        put(1, mm(top[:, :own], act[2]) + mm(top[:, own:], rim[:far, :mid]))
        put(2, mm(top[:, :own], act[3]) + mm(top[:, own:], rim[:far, mid:]))
        put(3, mm(left[:, :own], act[1]) + mm(left[:, own:], rim[far:, :mid]))
        put(6, mm(left[:, :own], act[3]) + mm(left[:, own:], rim[far:, mid:]))
        put(0, mm(corner[:, :own], act[3]) + mm(corner[:, own:], rim[:, mid:]))
        for slot, k in ((4, 0), (5, 1), (7, 2), (8, 3)):
            columns[rows, slot * mid : (slot + 1) * mid] = act[k, rows, :]
        c = mm(columns[rows, :], w_spatial[...]).astype(BF16)
        conv2[rows, :] = c
        cf = c.astype(F32)
        return s + sums(cf), q + sums(cf * cf)

    z = jnp.zeros((1, mid), F32)
    s, q = lax.fori_loop(0, own // BLOCK, step, (z, z))
    mom[...] = jnp.zeros_like(mom)
    mom[0:1, :mid] = s
    mom[1:2, :mid] = q


def conv3_kernel(members, conv2, tot2, gm, sm, w_expand, act2, conv3, mom):
    mid = conv2.shape[1]
    center, inv = norm_of(tot2[...], 0, mid, members)

    def step(i, carry):
        s, q = carry
        rows = block(i, BLOCK)
        v = (conv2[rows, :].astype(F32) - center) * inv
        a = smooth(v * gm[1:2] + sm[1:2]).astype(BF16)
        act2[rows, :] = a
        c = mm(a, w_expand[...]).astype(BF16)
        conv3[rows, :] = c
        cf = c.astype(F32)
        return s + sums(cf), q + sums(cf * cf)

    z = jnp.zeros((1, conv3.shape[1]), F32)
    s, q = lax.fori_loop(0, conv2.shape[0] // BLOCK, step, (z, z))
    mom[...] = jnp.zeros_like(mom)
    mom[0:1, :] = s
    mom[1:2, :] = q


def result_kernel(
    members, conv3, conv_short, tot3, tot1, gw, sw, dst, dst_t, cot, up, outgoing, mom, res
):
    wide = conv3.shape[1]
    rows_all = conv3.shape[0]
    slots = cot.shape[0]
    c3, i3 = norm_of(tot3[...], 0, wide, members)
    cs, is_ = norm_of(tot1[...], 2, wide, members)

    def step(i, carry):
        a, b, c = carry
        rows = block(i, BLOCK)
        n3 = (conv3[rows, :].astype(F32) - c3) * i3
        ns = (conv_short[rows, :].astype(F32) - cs) * is_
        summed = n3 * gw[0:1] + sw[0:1] + (ns * gw[1:2] + sw[1:2])
        res[rows, :] = smooth(summed).astype(BF16)
        picked = mm(onehot(dst[rows, :], 1, (BLOCK, slots)), cot[...])
        u = picked * slope(summed)
        up[rows, :] = u
        return a + sums(u), b + sums(u * n3), c + sums(u * ns)

    z = jnp.zeros((1, wide), F32)
    a, b, c = lax.fori_loop(0, rows_all // BLOCK, step, (z, z, z))
    mom[...] = jnp.zeros_like(mom)
    mom[0:1, :] = a
    mom[1:2, :] = b
    mom[2:3, :] = c

    def send(i, _):
        at = dst_t[...] - i * BLOCK
        outgoing[block(i, BLOCK), :] = mm(onehot(at, 0, (BLOCK, rows_all)), res[...]).astype(BF16)
        return 0

    lax.fori_loop(0, slots // BLOCK, send, 0)


def back3_kernel(
    wide_members,
    mid_members,
    up,
    conv3,
    conv_short,
    tot3,
    tot1,
    totb,
    gw,
    act2,
    sub_in,
    conv2,
    tot2,
    gm,
    sm,
    w_expand,
    dshort,
    g_expand,
    g_short,
    back2,
    mom,
    d3,
):
    wide = conv3.shape[1]
    mid = conv2.shape[1]
    rows_all = conv3.shape[0]
    c3, i3 = norm_of(tot3[...], 0, wide, wide_members)
    cs, is_ = norm_of(tot1[...], 2, wide, wide_members)
    f3, h3 = back_of(totb[...], 0, 1, gw[0:1], wide, wide_members)
    fs, hs = back_of(totb[...], 0, 2, gw[1:2], wide, wide_members)
    c2, i2 = norm_of(tot2[...], 0, mid, mid_members)

    def step(i, carry):
        s, q = carry
        rows = block(i, BLOCK)
        u = up[rows, :]
        n3 = (conv3[rows, :].astype(F32) - c3) * i3
        ns = (conv_short[rows, :].astype(F32) - cs) * is_
        d = (i3 * (gw[0:1] * u - f3 - n3 * h3)).astype(BF16)
        d3[rows, :] = d
        dshort[rows, :] = (is_ * (gw[1:2] * u - fs - ns * hs)).astype(BF16)
        n2 = (conv2[rows, :].astype(F32) - c2) * i2
        b = mm_t(d, w_expand[...]) * slope(n2 * gm[1:2] + sm[1:2])
        back2[rows, :] = b
        return s + sums(b), q + sums(b * n2)

    z = jnp.zeros((1, mid), F32)
    s, q = lax.fori_loop(0, rows_all // BLOCK, step, (z, z))
    mom[...] = jnp.zeros_like(mom)
    mom[0:1, :mid] = s
    mom[1:2, :mid] = q
    g_expand[...] = t_mm(act2[...], d3[...]).astype(BF16)

    for j in range(wide // BLOCK):
        cut = slice(j * BLOCK, (j + 1) * BLOCK)
        g_short[cut, :] = t_mm(sub_in[:, cut], dshort[...]).astype(BF16)


def back2_kernel(
    members,
    back2,
    conv2,
    tot2,
    totb,
    gm,
    columns,
    src_t,
    w_spatial,
    rims,
    g_spatial,
    planes,
    rim,
    d2,
):
    mid = conv2.shape[1]
    own = conv2.shape[0]
    far = rims // 2
    c2, i2 = norm_of(tot2[...], 0, mid, members)
    f2, h2 = back_of(totb[...], 0, 1, gm[1:2], mid, members)
    n2 = (conv2[...].astype(F32) - c2) * i2
    d2[...] = (i2 * (gm[1:2] * back2[...] - f2 - n2 * h2)).astype(BF16)
    d = d2[...]

    def part(slot):
        return mm_t(d, w_spatial[slot * mid : (slot + 1) * mid, :])

    for slot in range(9):
        cut = slice(slot * mid, (slot + 1) * mid)
        g_spatial[cut, :] = t_mm(columns[:, cut], d).astype(BF16)
    top_a, top_b = part(1).astype(BF16), part(2).astype(BF16)
    left_a, left_b = part(3).astype(BF16), part(6).astype(BF16)
    corner = part(0).astype(BF16)
    planes[0] = part(4)
    planes[1] = part(5)
    planes[2] = part(7)
    planes[3] = part(8)
    top_at, left_at, corner_at = src_t[0:1, :], src_t[1:2, :], src_t[2:3, :]

    def step(i, _):
        rows = block(i, BLOCK)
        top = onehot(top_at - i * BLOCK, 0, (BLOCK, own))
        left = onehot(left_at - i * BLOCK, 0, (BLOCK, own))
        both = onehot(corner_at - i * BLOCK, 0, (BLOCK, own))
        planes[1, rows, :] += mm(left, left_a)
        planes[2, rows, :] += mm(top, top_a)
        planes[3, rows, :] += mm(top, top_b) + mm(left, left_b) + mm(both, corner)
        return 0

    lax.fori_loop(0, own // BLOCK, step, 0)
    top = onehot(top_at - own, 0, (far, own))
    left = onehot(left_at - own, 0, (far, own))
    over = onehot(corner_at - own, 0, (far, own))
    beside = onehot(corner_at - own - far, 0, (far, own))
    rim[:far, :mid] = mm(top, top_a).astype(BF16)
    rim[:far, mid:] = (mm(top, top_b) + mm(over, corner)).astype(BF16)
    rim[far:, :mid] = mm(left, left_a).astype(BF16)
    rim[far:, mid:] = (mm(left, left_b) + mm(beside, corner)).astype(BF16)


def back1_kernel(members, planes, rim, ends, conv1, tot1, gm, sm, back1, mom):
    mid = conv1.shape[2]
    far = ends.shape[0] // 2
    center, inv = norm_of(tot1[...], 0, mid, members)
    s = q = jnp.zeros((1, mid), F32)
    for k in range(4):
        v = planes[k]
        if k >= 2:
            v = v + t_mm(ends[:far, :], rim[:far, (k - 2) * mid : (k - 1) * mid])
        if k % 2:
            lane = k // 2
            v = v + t_mm(ends[far:, :], rim[far:, lane * mid : (lane + 1) * mid])
        n = (conv1[k].astype(F32) - center) * inv
        b = v * slope(n * gm[0:1] + sm[0:1])
        back1[k] = b
        s, q = s + sums(b), q + sums(b * n)
    mom[...] = jnp.zeros_like(mom)
    mom[0:1, :mid] = s
    mom[1:2, :mid] = q


def last_kernel(
    members,
    back1,
    conv1,
    tot1,
    totb,
    gm,
    feat,
    w_reduce,
    dshort,
    w_short,
    sel_t,
    g_feat,
    g_reduce,
    total,
):
    mid = conv1.shape[2]
    rows = STEP * SIDE * SIDE
    part = STEP * Q
    center, inv = norm_of(tot1[...], 0, mid, members)
    first, second = back_of(totb[...], 0, 1, gm[0:1], mid, members)
    total[...] = jnp.zeros_like(total)

    def step(g, _):
        cuts = []
        for k in range(4):
            n = (conv1[k, block(g, part), :].astype(F32) - center) * inv
            u = back1[k, block(g, part), :]
            cuts.append((inv * (gm[0:1] * u - first - n * second)).astype(BF16))
        d = jnp.concatenate(cuts, axis=0)
        total[...] += t_mm(feat[block(g, rows), :], mm(sel_t[...], d).astype(BF16))
        short = mm_t(dshort[block(g, part), :], w_short[...])
        back = mm_t(d, w_reduce[...])
        back = jnp.concatenate([back[:part] + short, back[part:]], axis=0).astype(BF16)
        g_feat[block(g, rows), :] = mm(sel_t[...], back).astype(BF16)
        return 0

    lax.fori_loop(0, feat.shape[0] // rows, step, 0)
    g_reduce[...] = total[...].astype(BF16)


def local(kernel, outs, scratch=()):
    vmem = pl.BlockSpec(memory_space=pltpu.VMEM)

    def call(*args):
        return pl.pallas_call(
            kernel,
            out_shape=[jax.ShapeDtypeStruct(s, t) for s, t in outs],
            in_specs=[vmem] * len(args),
            out_specs=[vmem] * len(outs),
            scratch_shapes=[pltpu.VMEM(s, t) for s, t in scratch],
            compiler_params=pltpu.CompilerParams(vmem_limit_bytes=40 * 1024 * 1024),
        )(*args)

    return call


def sum_kernel(peers, x, out, slots, send, recv):
    me = lax.axis_index("space")
    barrier = pltpu.get_barrier_semaphore()
    for k in range(1, peers):
        pl.semaphore_signal(
            barrier, inc=1, device_id={"space": lax.rem(me + k, peers)}, device_id_type=MESH
        )
    slots[0] = x[...]
    pl.semaphore_wait(barrier, peers - 1)
    copies = []
    for k in range(1, peers):
        copy = pltpu.make_async_remote_copy(
            src_ref=x,
            dst_ref=slots.at[k],
            send_sem=send.at[k],
            recv_sem=recv.at[k],
            device_id={"space": lax.rem(me + k, peers)},
            device_id_type=MESH,
        )
        copy.start()
        copies.append(copy)
    for copy in copies:
        copy.wait()
    total = slots[me]
    for s in range(1, peers):
        total = total + slots[lax.rem(me - s + peers, peers)]
    out[...] = total


def slide_total(table):
    peers = lax.axis_size("space")
    vmem = pl.BlockSpec(memory_space=pltpu.VMEM)
    return pl.pallas_call(
        functools.partial(sum_kernel, peers),
        out_shape=jax.ShapeDtypeStruct(table.shape, F32),
        in_specs=[vmem],
        out_specs=vmem,
        scratch_shapes=[
            pltpu.VMEM((peers,) + table.shape, F32),
            pltpu.SemaphoreType.DMA((peers,)),
            pltpu.SemaphoreType.DMA((peers,)),
        ],
        compiler_params=pltpu.CompilerParams(collective_id=1, has_side_effects=True),
    )(table)


def share_kernel(
    groups, peers, w, vec, out, vec_out, in1, inv, mid, in2, done, in3, s1, r1, sv, rv, s2, r2, s3, r3
):
    d = lax.axis_index("dp")
    me = lax.axis_index("space")
    barrier = pltpu.get_barrier_semaphore()
    for k in range(1, groups):
        pl.semaphore_signal(
            barrier, inc=1, device_id={"dp": lax.rem(d + k, groups)}, device_id_type=MESH
        )
    for k in range(1, peers):
        pl.semaphore_signal(
            barrier, inc=1, device_id={"space": lax.rem(me + k, peers)}, device_id_type=MESH
        )
    inv[0] = vec[...]
    pl.semaphore_wait(barrier, groups + peers - 2)

    def across(k, src, dst, send, recv):
        copy = pltpu.make_async_remote_copy(
            src_ref=src,
            dst_ref=dst,
            send_sem=send.at[k],
            recv_sem=recv.at[k],
            device_id={"dp": lax.rem(d + k, groups)},
            device_id_type=MESH,
        )
        copy.start()
        return copy

    copies = []
    for k in range(1, groups):
        copies.append(across(k, w.at[lax.rem(d + k, groups)], in1.at[k], s1, r1))
        copies.append(across(k, vec, inv.at[k], sv, rv))
    for copy in copies:
        copy.wait()

    def add(i, _):
        total = w[d, i].astype(F32)
        for k in range(1, groups):
            total = total + in1[k, i].astype(F32)
        mid[i] = total.astype(BF16)
        return 0

    lax.fori_loop(0, peers, add, 0)
    copies = []
    for k in range(1, peers):
        to = lax.rem(me + k, peers)
        copy = pltpu.make_async_remote_copy(
            src_ref=mid.at[to],
            dst_ref=in2.at[k],
            send_sem=s2.at[k],
            recv_sem=r2.at[k],
            device_id={"space": to},
            device_id_type=MESH,
        )
        copy.start()
        copies.append(copy)
    total = inv[d]
    for s in range(1, groups):
        total = total + inv[lax.rem(d - s + groups, groups)]
    vec_out[...] = total
    for copy in copies:
        copy.wait()
    total = mid[me].astype(F32)
    for k in range(1, peers):
        total = total + in2[k].astype(F32)
    done[...] = total.astype(BF16)
    copies = [across(k, done, in3.at[k], s3, r3) for k in range(1, groups)]
    out[d] = done[...].astype(F32)
    for k, copy in enumerate(copies):
        copy.wait()
        out[lax.rem(d - k - 1 + groups, groups)] = in3[k + 1].astype(F32)


def share_total(w, vec):
    groups, peers = lax.axis_size("dp"), lax.axis_size("space")
    piece = w.shape[2:]
    vmem = pl.BlockSpec(memory_space=pltpu.VMEM)
    dma = pltpu.SemaphoreType.DMA
    return pl.pallas_call(
        functools.partial(share_kernel, groups, peers),
        out_shape=[
            jax.ShapeDtypeStruct((groups,) + piece, F32),
            jax.ShapeDtypeStruct(vec.shape, F32),
        ],
        in_specs=[vmem] * 2,
        out_specs=[vmem] * 2,
        scratch_shapes=[
            pltpu.VMEM(w.shape, BF16),
            pltpu.VMEM((groups,) + vec.shape, F32),
            pltpu.VMEM((peers,) + piece, BF16),
            pltpu.VMEM((peers,) + piece, BF16),
            pltpu.VMEM(piece, BF16),
            pltpu.VMEM((groups,) + piece, BF16),
            dma((groups,)),
            dma((groups,)),
            dma((groups,)),
            dma((groups,)),
            dma((peers,)),
            dma((peers,)),
            dma((groups,)),
            dma((groups,)),
        ],
        compiler_params=pltpu.CompilerParams(
            collective_id=2, has_side_effects=True, vmem_limit_bytes=24 * 1024 * 1024
        ),
    )(w, vec)


def passed_along(shard, by):
    peers = lax.axis_size("space")
    pairs = [(i, i + by) for i in range(peers) if 0 <= i + by < peers]
    return lax.ppermute(shard, "space", pairs)


def source_rows(links, me, tiles):
    own = tiles * Q
    t = jnp.arange(tiles, dtype=jnp.int32)[:, None, None]
    i = jnp.arange(HALF, dtype=jnp.int32)[None, :, None]
    j = jnp.arange(HALF, dtype=jnp.int32)[None, None, :]
    last = HALF - 1
    far = tiles * HALF

    def away(column, r, c, along, base):
        index = links[:, column][:, None, None]
        at = index - me * tiles
        here = at * Q + r * HALF + c
        there = own + base + (at + tiles) * HALF + along
        return jnp.where(index < 0, -1, jnp.where(at >= 0, here, there))

    top = jnp.where(i > 0, t * Q + (i - 1) * HALF + j, away(0, last, j, j, 0))
    left = jnp.where(j > 0, t * Q + i * HALF + j - 1, away(1, i, last, i, 0))
    corner = jnp.where(
        i > 0,
        jnp.where(
            j > 0, t * Q + (i - 1) * HALF + j - 1, away(1, i - 1, last, i - 1, far)
        ),
        jnp.where(j > 0, away(0, last, j - 1, j - 1, 0), away(2, last, last, last, 0)),
    )
    return jnp.stack([jnp.broadcast_to(x, (tiles, HALF, HALF)).reshape(own) for x in (top, left, corner)])


def plane_order():
    order = np.zeros((STEP * SIDE * SIDE, STEP * SIDE * SIDE), np.float32)
    row = 0
    for a in range(2):
        for b in range(2):
            for t in range(STEP):
                for i in range(HALF):
                    for j in range(HALF):
                        order[row, t * SIDE * SIDE + (2 * i + a) * SIDE + 2 * j + b] = 1
                        row += 1
    return order


def rim_rows(tiles):
    ends = np.zeros((2, tiles, HALF, tiles, HALF, HALF), np.float32)
    for t in range(tiles):
        for j in range(HALF):
            ends[0, t, j, t, HALF - 1, j] = 1
            ends[1, t, j, t, j, HALF - 1] = 1
    return ends.reshape(2 * tiles * HALF, tiles * Q)


def body(
    features,
    owners,
    neighbors,
    w_reduce,
    w_spatial,
    w_expand,
    w_short,
    gm,
    sm,
    gw,
    sw,
    cotangent,
):
    spaces = lax.axis_size("space")
    groups = lax.axis_size("dp")
    me = lax.axis_index("space")
    tiles = features.shape[1]
    wide = features.shape[3]
    mid = w_reduce.shape[1]
    tiles_total = tiles * spaces
    slides = features.shape[0] * groups
    capacity = cotangent.shape[1] // spaces
    slots = spaces * capacity * Q
    own = tiles * Q
    rims = 2 * tiles * HALF
    m_in = float(tiles_total * SIDE * SIDE * (mid // GROUPS))
    m_mid = float(tiles_total * Q * (mid // GROUPS))
    m_wide = float(tiles_total * Q * (wide // GROUPS))
    table = ((8, wide), F32)

    cot_home = lax.all_to_all(
        cotangent[0].reshape(spaces, capacity * Q, wide), "space", split_axis=0, concat_axis=0, tiled=True
    ).reshape(slots, wide)
    order = plane_order()
    sel, sel_t = jnp.asarray(order, BF16), jnp.asarray(order.T, BF16)
    ends = jnp.asarray(rim_rows(tiles), BF16)
    src_t = source_rows(neighbors[0], me, tiles)
    src = src_t.T
    owner_of = owners[0][:, 0]
    earlier = jnp.arange(tiles)[None, :] < jnp.arange(tiles)[:, None]
    same = (owner_of[:, None] == owner_of[None, :]) & earlier
    slot_of = owner_of * capacity + jnp.sum(same.astype(jnp.int32), axis=1)
    dst = (slot_of[:, None] * Q + jnp.arange(Q, dtype=jnp.int32)[None, :]).reshape(own)
    feat = features[0].reshape(tiles * SIDE * SIDE, wide)

    conv1, sub_in, conv_short, mom = local(
        first_kernel,
        [((4, own, mid), BF16), ((own, wide), BF16), ((own, wide), BF16), table],
    )(feat, w_reduce, w_short, sel)
    tot1 = slide_total(mom)
    act, rim = local(
        functools.partial(act_kernel, m_in), [((4, own, mid), BF16), ((rims, 2 * mid), BF16)]
    )(conv1, tot1, gm, sm, ends)
    prior = passed_along(rim, 1)
    columns, conv2, mom = local(
        conv2_kernel, [((own, 9 * mid), BF16), ((own, mid), BF16), table]
    )(act, prior, src, w_spatial)
    tot2 = slide_total(mom)
    act2, conv3, mom = local(
        functools.partial(conv3_kernel, m_mid), [((own, mid), BF16), ((own, wide), BF16), table]
    )(conv2, tot2, gm, sm, w_expand)
    tot3 = slide_total(mom)
    up, outgoing, mom = local(
        functools.partial(result_kernel, m_wide),
        [((own, wide), F32), ((slots, wide), BF16), table],
        [((own, wide), BF16)],
    )(conv3, conv_short, tot3, tot1, gw, sw, dst[:, None], dst[None, :], cot_home)
    arrived = lax.all_to_all(
        outgoing.reshape(spaces, capacity * Q, wide), "space", split_axis=0, concat_axis=0, tiled=True
    )
    block_out = arrived.reshape(1, spaces * capacity, Q, wide)
    tot3b = slide_total(mom)
    dshort, g_expand, g_short, back2, mom = local(
        functools.partial(back3_kernel, m_wide, m_mid),
        [
            ((own, wide), BF16),
            ((mid, wide), BF16),
            ((wide, wide), BF16),
            ((own, mid), F32),
            table,
        ],
        [((own, wide), BF16)],
    )(up, conv3, conv_short, tot3, tot1, tot3b, gw, act2, sub_in, conv2, tot2, gm, sm, w_expand)
    tot2b = slide_total(mom)

    def back2_entry(a, b, c, d, e, f, g, h, *rest):
        back2_kernel(m_mid, a, b, c, d, e, f, g, h, rims, *rest)

    g_spatial, planes, rim = local(
        back2_entry,
        [((9 * mid, mid), BF16), ((4, own, mid), F32), ((rims, 2 * mid), BF16)],
        [((own, mid), BF16)],
    )(back2, conv2, tot2, tot2b, gm, columns, src_t, w_spatial)
    following = passed_along(rim, -1)
    back1, mom = local(
        functools.partial(back1_kernel, m_in), [((4, own, mid), F32), table]
    )(planes, following, ends, conv1, tot1, gm, sm)
    tot1b = slide_total(mom)
    g_feat, g_reduce = local(
        functools.partial(last_kernel, m_in),
        [((tiles * SIDE * SIDE, wide), BF16), ((wide, mid), BF16)],
        [((wide, mid), F32)],
    )(back1, conv1, tot1, tot1b, gm, feat, w_reduce, dshort, w_short, sel_t)

    lanes = mid

    def cut(g):
        share = g.shape[0] // spaces
        wide_by = g.shape[1] // lanes
        g = g.reshape(spaces, share, wide_by, lanes).transpose(0, 2, 1, 3)
        return g.reshape(spaces, share * wide_by, lanes)

    parts = [cut(g) for g in (g_reduce, g_spatial, g_expand, g_short)]
    counts = [p.shape[1] for p in parts]
    piece = -(-sum(counts) // (groups * 16)) * 16
    filler = jnp.zeros((spaces, groups * piece - sum(counts), lanes), BF16)
    packed = jnp.concatenate(parts + [filler], axis=1)
    packed = packed.reshape(spaces, groups, piece, lanes).transpose(1, 0, 2, 3)
    vec = jnp.concatenate(
        [
            jnp.concatenate([tot1b[:2, :mid], tot2b[:2, :mid]], axis=1),
            jnp.zeros((2, wide - 2 * mid), F32),
        ],
        axis=1,
    )
    vec = jnp.concatenate([vec, tot3b[:3], jnp.zeros((3, wide), F32)], axis=0)
    shares, sums_dp = share_total(packed, vec)
    shares = shares.reshape(groups * piece, lanes)
    scale_in = 1.0 / math.sqrt(slides * tiles_total * SIDE * SIDE)
    scale_out = 1.0 / math.sqrt(slides * tiles_total * Q)

    def uncut(at, count, columns_by):
        g = shares[at : at + count].reshape(columns_by, count // columns_by, lanes)
        return g.transpose(1, 0, 2).reshape(count // columns_by, columns_by * lanes)

    def own_part(a):
        share = a.shape[1] // spaces
        return lax.dynamic_slice_in_dim(a, me * share, share, 1)

    at = [0]
    for c in counts:
        at.append(at[-1] + c)
    mid_scale = jnp.array([[scale_in], [scale_out]], F32)
    return (
        block_out,
        g_feat.reshape(1, tiles, SIDE * SIDE, wide),
        uncut(at[0], counts[0], 1) * scale_in,
        uncut(at[1], counts[1], 1) * scale_out,
        uncut(at[2], counts[2], wide // lanes) * scale_out,
        uncut(at[3], counts[3], wide // lanes) * scale_out,
        own_part(jnp.stack([sums_dp[1, :mid], sums_dp[1, mid : 2 * mid]])) * mid_scale,
        own_part(jnp.stack([sums_dp[0, :mid], sums_dp[0, mid : 2 * mid]])) * mid_scale,
        own_part(sums_dp[3:5]) * scale_out,
        own_part(jnp.stack([sums_dp[2], sums_dp[2]])) * scale_out,
    )


def solution(mesh):
    placed = (
        P("dp", "space", None, None),
        P("dp", "space", None),
        P("dp", "space", None),
        P(),
        P(),
        P(),
        P(),
        P(),
        P(),
        P(),
        P(),
        P("dp", "space", None, None),
    )
    return jax.shard_map(
        body,
        mesh=mesh,
        in_specs=placed,
        out_specs=(
            P("dp", "space", None, None),
            P("dp", "space", None, None),
            P("space", None),
            P("space", None),
            P("space", None),
            P("space", None),
            P(None, "space"),
            P(None, "space"),
            P(None, "space"),
            P(None, "space"),
        ),
        check_vma=False,
    )
```

```python
import functools
import math

import jax
import jax.numpy as jnp
import numpy as np
from jax import lax
from jax.experimental import pallas as pl
from jax.experimental.pallas import tpu as pltpu
from jax.sharding import PartitionSpec as P

GROUPS = 32
SIDE = 8
HALF = SIDE // 2
Q = HALF * HALF
EPS = 1e-05
MESH = pl.DeviceIdType.MESH
F32 = jnp.float32
BF16 = jnp.bfloat16
STEP = 4
BLOCK = 128


def sigmoid(v):
    return 1.0 / (1.0 + jnp.exp(-v))


def smooth(v):
    return v * sigmoid(v)


def slope(v):
    s = sigmoid(v)
    return s * (1.0 + v * (1.0 - s))


def mm(a, b):
    return lax.dot_general(a, b, (((1,), (0,)), ((), ())), preferred_element_type=F32)


def mm_t(a, b):
    return lax.dot_general(a, b, (((1,), (1,)), ((), ())), preferred_element_type=F32)


def t_mm(a, b):
    return lax.dot_general(a, b, (((0,), (0,)), ((), ())), preferred_element_type=F32)


def group_sum(rows):
    width = rows.shape[-1]
    each = width // GROUPS
    a = lax.broadcasted_iota(jnp.int32, (width, width), 0) // each
    b = lax.broadcasted_iota(jnp.int32, (width, width), 1) // each
    same = jnp.where(a == b, 1.0, 0.0).astype(F32)
    return lax.dot_general(
        rows,
        same,
        (((1,), (0,)), ((), ())),
        precision=lax.Precision.HIGHEST,
        preferred_element_type=F32,
    )


def norm_of(tot, first, width, members):
    g = group_sum(tot[:, :width])
    center = g[first : first + 1] / members
    spread = g[first + 1 : first + 2] / members - center * center
    return center, lax.rsqrt(spread + EPS)


def back_of(tot, first, second, gain, width, members):
    g = group_sum(tot[:, :width] * gain)
    return g[first : first + 1] / members, g[second : second + 1] / members


def sums(v):
    return jnp.sum(v, axis=0, keepdims=True)


def onehot(index, axis, shape):
    return jnp.where(lax.broadcasted_iota(jnp.int32, shape, axis) == index, 1.0, 0.0).astype(BF16)


def block(i, size):
    start = i * size
    return pl.ds(start if isinstance(start, int) else pl.multiple_of(start, size), size)


def first_kernel(feat, w_reduce, w_short, sel, conv1, sub_in, conv_short, mom):
    rows = STEP * SIDE * SIDE
    part = STEP * Q
    wide = w_short.shape[1]
    mid = w_reduce.shape[1]

    def step(g, carry):
        s1, q1, s2, q2 = carry
        x = feat[block(g, rows), :]
        c = mm(x, w_reduce[...]).astype(BF16)
        cf = c.astype(F32)
        p = mm(sel[...], c).astype(BF16)
        for k in range(4):
            conv1[k, block(g, part), :] = p[k * part : (k + 1) * part]
        sub = mm(sel[:part, :], x).astype(BF16)
        sub_in[block(g, part), :] = sub
        sh = mm(sub, w_short[...]).astype(BF16)
        conv_short[block(g, part), :] = sh
        sf = sh.astype(F32)
        return s1 + sums(cf), q1 + sums(cf * cf), s2 + sums(sf), q2 + sums(sf * sf)

    z1, z2 = jnp.zeros((1, mid), F32), jnp.zeros((1, wide), F32)
    s1, q1, s2, q2 = lax.fori_loop(0, feat.shape[0] // rows, step, (z1, z1, z2, z2))
    mom[...] = jnp.zeros_like(mom)
    mom[0:1, :mid] = s1
    mom[1:2, :mid] = q1
    mom[2:3, :] = s2
    mom[3:4, :] = q2


def act_kernel(members, conv1, tot1, gm, sm, ends, act, rim):
    mid = conv1.shape[2]
    center, inv = norm_of(tot1[...], 0, mid, members)
    for k in range(4):

        def step(i, _, k=k):
            v = (conv1[k, block(i, BLOCK), :].astype(F32) - center) * inv
            act[k, block(i, BLOCK), :] = smooth(v * gm[0:1] + sm[0:1]).astype(BF16)
            return 0

        lax.fori_loop(0, conv1.shape[1] // BLOCK, step, 0)
    count = ends.shape[0] // 2
    for k, e, lane in ((2, 0, 0), (3, 0, 1), (1, 1, 0), (3, 1, 1)):
        rim[e * count : (e + 1) * count, lane * mid : (lane + 1) * mid] = mm(
            ends[e * count : (e + 1) * count, :], act[k]
        ).astype(BF16)


def conv2_kernel(act, rim, src, w_spatial, columns, conv2, mom):
    mid = act.shape[2]
    own = act.shape[1]
    far = rim.shape[0] // 2

    def step(i, carry):
        s, q = carry
        rows = block(i, BLOCK)
        at = src[rows, :]
        top = onehot(at[:, 0:1], 1, (BLOCK, own + far))
        left = onehot(at[:, 1:2], 1, (BLOCK, own + far))
        corner = onehot(at[:, 2:3], 1, (BLOCK, own + 2 * far))

        def put(slot, v):
            columns[rows, slot * mid : (slot + 1) * mid] = v.astype(BF16)

        put(1, mm(top[:, :own], act[2]) + mm(top[:, own:], rim[:far, :mid]))
        put(2, mm(top[:, :own], act[3]) + mm(top[:, own:], rim[:far, mid:]))
        put(3, mm(left[:, :own], act[1]) + mm(left[:, own:], rim[far:, :mid]))
        put(6, mm(left[:, :own], act[3]) + mm(left[:, own:], rim[far:, mid:]))
        put(0, mm(corner[:, :own], act[3]) + mm(corner[:, own:], rim[:, mid:]))
        for slot, k in ((4, 0), (5, 1), (7, 2), (8, 3)):
            columns[rows, slot * mid : (slot + 1) * mid] = act[k, rows, :]
        c = mm(columns[rows, :], w_spatial[...]).astype(BF16)
        conv2[rows, :] = c
        cf = c.astype(F32)
        return s + sums(cf), q + sums(cf * cf)

    z = jnp.zeros((1, mid), F32)
    s, q = lax.fori_loop(0, own // BLOCK, step, (z, z))
    mom[...] = jnp.zeros_like(mom)
    mom[0:1, :mid] = s
    mom[1:2, :mid] = q


def conv3_kernel(members, conv2, tot2, gm, sm, w_expand, act2, conv3, mom):
    mid = conv2.shape[1]
    center, inv = norm_of(tot2[...], 0, mid, members)

    def step(i, carry):
        s, q = carry
        rows = block(i, BLOCK)
        v = (conv2[rows, :].astype(F32) - center) * inv
        a = smooth(v * gm[1:2] + sm[1:2]).astype(BF16)
        act2[rows, :] = a
        c = mm(a, w_expand[...]).astype(BF16)
        conv3[rows, :] = c
        cf = c.astype(F32)
        return s + sums(cf), q + sums(cf * cf)

    z = jnp.zeros((1, conv3.shape[1]), F32)
    s, q = lax.fori_loop(0, conv2.shape[0] // BLOCK, step, (z, z))
    mom[...] = jnp.zeros_like(mom)
    mom[0:1, :] = s
    mom[1:2, :] = q


def result_kernel(
    members, conv3, conv_short, tot3, tot1, gw, sw, dst, dst_t, cot, up, outgoing, mom, res
):
    wide = conv3.shape[1]
    rows_all = conv3.shape[0]
    slots = cot.shape[0]
    c3, i3 = norm_of(tot3[...], 0, wide, members)
    cs, is_ = norm_of(tot1[...], 2, wide, members)

    def step(i, carry):
        a, b, c = carry
        rows = block(i, BLOCK)
        n3 = (conv3[rows, :].astype(F32) - c3) * i3
        ns = (conv_short[rows, :].astype(F32) - cs) * is_
        summed = n3 * gw[0:1] + sw[0:1] + (ns * gw[1:2] + sw[1:2])
        res[rows, :] = smooth(summed).astype(BF16)
        picked = mm(onehot(dst[rows, :], 1, (BLOCK, slots)), cot[...])
        u = picked * slope(summed)
        up[rows, :] = u
        return a + sums(u), b + sums(u * n3), c + sums(u * ns)

    z = jnp.zeros((1, wide), F32)
    a, b, c = lax.fori_loop(0, rows_all // BLOCK, step, (z, z, z))
    mom[...] = jnp.zeros_like(mom)
    mom[0:1, :] = a
    mom[1:2, :] = b
    mom[2:3, :] = c

    def send(i, _):
        at = dst_t[...] - i * BLOCK
        outgoing[block(i, BLOCK), :] = mm(onehot(at, 0, (BLOCK, rows_all)), res[...]).astype(BF16)
        return 0

    lax.fori_loop(0, slots // BLOCK, send, 0)


def back3_kernel(
    wide_members,
    mid_members,
    up,
    conv3,
    conv_short,
    tot3,
    tot1,
    totb,
    gw,
    act2,
    sub_in,
    conv2,
    tot2,
    gm,
    sm,
    w_expand,
    dshort,
    g_expand,
    g_short,
    back2,
    mom,
    d3,
):
    wide = conv3.shape[1]
    mid = conv2.shape[1]
    rows_all = conv3.shape[0]
    c3, i3 = norm_of(tot3[...], 0, wide, wide_members)
    cs, is_ = norm_of(tot1[...], 2, wide, wide_members)
    f3, h3 = back_of(totb[...], 0, 1, gw[0:1], wide, wide_members)
    fs, hs = back_of(totb[...], 0, 2, gw[1:2], wide, wide_members)
    c2, i2 = norm_of(tot2[...], 0, mid, mid_members)

    def step(i, carry):
        s, q = carry
        rows = block(i, BLOCK)
        u = up[rows, :]
        n3 = (conv3[rows, :].astype(F32) - c3) * i3
        ns = (conv_short[rows, :].astype(F32) - cs) * is_
        d = (i3 * (gw[0:1] * u - f3 - n3 * h3)).astype(BF16)
        d3[rows, :] = d
        dshort[rows, :] = (is_ * (gw[1:2] * u - fs - ns * hs)).astype(BF16)
        n2 = (conv2[rows, :].astype(F32) - c2) * i2
        b = mm_t(d, w_expand[...]) * slope(n2 * gm[1:2] + sm[1:2])
        back2[rows, :] = b
        return s + sums(b), q + sums(b * n2)

    z = jnp.zeros((1, mid), F32)
    s, q = lax.fori_loop(0, rows_all // BLOCK, step, (z, z))
    mom[...] = jnp.zeros_like(mom)
    mom[0:1, :mid] = s
    mom[1:2, :mid] = q
    g_expand[...] = t_mm(act2[...], d3[...]).astype(BF16)

    for j in range(wide // BLOCK):
        cut = slice(j * BLOCK, (j + 1) * BLOCK)
        g_short[cut, :] = t_mm(sub_in[:, cut], dshort[...]).astype(BF16)


def back2_kernel(
    members,
    back2,
    conv2,
    tot2,
    totb,
    gm,
    columns,
    src_t,
    w_spatial,
    rims,
    g_spatial,
    planes,
    rim,
    d2,
):
    mid = conv2.shape[1]
    own = conv2.shape[0]
    far = rims // 2
    c2, i2 = norm_of(tot2[...], 0, mid, members)
    f2, h2 = back_of(totb[...], 0, 1, gm[1:2], mid, members)
    n2 = (conv2[...].astype(F32) - c2) * i2
    d2[...] = (i2 * (gm[1:2] * back2[...] - f2 - n2 * h2)).astype(BF16)
    d = d2[...]

    def part(slot):
        return mm_t(d, w_spatial[slot * mid : (slot + 1) * mid, :])

    for slot in range(9):
        cut = slice(slot * mid, (slot + 1) * mid)
        g_spatial[cut, :] = t_mm(columns[:, cut], d).astype(BF16)
    top_a, top_b = part(1).astype(BF16), part(2).astype(BF16)
    left_a, left_b = part(3).astype(BF16), part(6).astype(BF16)
    corner = part(0).astype(BF16)
    planes[0] = part(4)
    planes[1] = part(5)
    planes[2] = part(7)
    planes[3] = part(8)
    top_at, left_at, corner_at = src_t[0:1, :], src_t[1:2, :], src_t[2:3, :]

    def step(i, _):
        rows = block(i, BLOCK)
        top = onehot(top_at - i * BLOCK, 0, (BLOCK, own))
        left = onehot(left_at - i * BLOCK, 0, (BLOCK, own))
        both = onehot(corner_at - i * BLOCK, 0, (BLOCK, own))
        planes[1, rows, :] += mm(left, left_a)
        planes[2, rows, :] += mm(top, top_a)
        planes[3, rows, :] += mm(top, top_b) + mm(left, left_b) + mm(both, corner)
        return 0

    lax.fori_loop(0, own // BLOCK, step, 0)
    top = onehot(top_at - own, 0, (far, own))
    left = onehot(left_at - own, 0, (far, own))
    over = onehot(corner_at - own, 0, (far, own))
    beside = onehot(corner_at - own - far, 0, (far, own))
    rim[:far, :mid] = mm(top, top_a).astype(BF16)
    rim[:far, mid:] = (mm(top, top_b) + mm(over, corner)).astype(BF16)
    rim[far:, :mid] = mm(left, left_a).astype(BF16)
    rim[far:, mid:] = (mm(left, left_b) + mm(beside, corner)).astype(BF16)


def back1_kernel(members, planes, rim, ends, conv1, tot1, gm, sm, back1, mom):
    mid = conv1.shape[2]
    far = ends.shape[0] // 2
    center, inv = norm_of(tot1[...], 0, mid, members)
    s = q = jnp.zeros((1, mid), F32)
    for k in range(4):
        v = planes[k]
        if k >= 2:
            v = v + t_mm(ends[:far, :], rim[:far, (k - 2) * mid : (k - 1) * mid])
        if k % 2:
            lane = k // 2
            v = v + t_mm(ends[far:, :], rim[far:, lane * mid : (lane + 1) * mid])
        n = (conv1[k].astype(F32) - center) * inv
        b = v * slope(n * gm[0:1] + sm[0:1])
        back1[k] = b
        s, q = s + sums(b), q + sums(b * n)
    mom[...] = jnp.zeros_like(mom)
    mom[0:1, :mid] = s
    mom[1:2, :mid] = q


def last_kernel(
    members,
    back1,
    conv1,
    tot1,
    totb,
    gm,
    feat,
    w_reduce,
    dshort,
    w_short,
    sel_t,
    g_feat,
    g_reduce,
    total,
):
    mid = conv1.shape[2]
    rows = STEP * SIDE * SIDE
    part = STEP * Q
    center, inv = norm_of(tot1[...], 0, mid, members)
    first, second = back_of(totb[...], 0, 1, gm[0:1], mid, members)
    total[...] = jnp.zeros_like(total)

    def step(g, _):
        cuts = []
        for k in range(4):
            n = (conv1[k, block(g, part), :].astype(F32) - center) * inv
            u = back1[k, block(g, part), :]
            cuts.append((inv * (gm[0:1] * u - first - n * second)).astype(BF16))
        d = jnp.concatenate(cuts, axis=0)
        total[...] += t_mm(feat[block(g, rows), :], mm(sel_t[...], d).astype(BF16))
        short = mm_t(dshort[block(g, part), :], w_short[...])
        back = mm_t(d, w_reduce[...])
        back = jnp.concatenate([back[:part] + short, back[part:]], axis=0).astype(BF16)
        g_feat[block(g, rows), :] = mm(sel_t[...], back).astype(BF16)
        return 0

    lax.fori_loop(0, feat.shape[0] // rows, step, 0)
    g_reduce[...] = total[...].astype(BF16)


def whole_kernel(members, peers, *refs):
    m_in, m_mid, m_wide = members
    (feat, cot, src, src_t, dst, dst_t, w_reduce, w_spatial, w_expand, w_short, gm, sm, gw, sw) = refs[:14]
    sel, sel_t, ends = refs[14:17]
    g_feat, landed, g_reduce, g_spatial, g_expand, g_short, tot = refs[17:24]
    (conv1, sub_in, conv_short, act, rim, prior, columns, conv2, act2, conv3) = refs[24:34]
    (up, outgoing, res, dshort, back2, d3, d2, planes, rim_b, following, back1) = refs[34:45]
    total, home, moms, slots = refs[45:49]
    sum_send, sum_recv, cot_send, cot_recv, out_send, out_recv, rim_send, rim_recv = refs[49:]
    me = lax.axis_index("space")
    barrier = pltpu.get_barrier_semaphore()
    for k in range(1, peers):
        pl.semaphore_signal(
            barrier, inc=1, device_id={"space": lax.rem(me + k, peers)}, device_id_type=MESH
        )
    pl.semaphore_wait(barrier, peers - 1)

    def send(by, source, target, out_sem, in_sem):
        copy = pltpu.make_async_remote_copy(
            src_ref=source,
            dst_ref=target,
            send_sem=out_sem,
            recv_sem=in_sem,
            device_id={"space": lax.rem(me + by, peers)},
            device_id_type=MESH,
        )
        copy.start()
        return copy

    def slide_total(n):
        copies = [
            send(k, moms.at[n], slots.at[n, k], sum_send.at[n, k], sum_recv.at[n, k])
            for k in range(1, peers)
        ]
        slots[n, 0] = moms[n]
        for copy in copies:
            copy.wait()
        sum_of = slots[n, me]
        for s in range(1, peers):
            sum_of = sum_of + slots[n, lax.rem(me - s + peers, peers)]
        tot[n] = sum_of

    rows = cot.shape[1]
    cot_copies = [
        send(k, cot.at[lax.rem(me + k, peers)], home.at[block(k, rows)], cot_send.at[k], cot_recv.at[k])
        for k in range(1, peers)
    ]
    first_kernel(feat, w_reduce, w_short, sel, conv1, sub_in, conv_short, moms.at[0])
    slide_total(0)
    act_kernel(m_in, conv1, tot.at[0], gm, sm, ends, act, rim)
    send(1, rim, prior, rim_send.at[0], rim_recv.at[0]).wait()
    conv2_kernel(act, prior, src, w_spatial, columns, conv2, moms.at[1])
    slide_total(1)
    conv3_kernel(m_mid, conv2, tot.at[1], gm, sm, w_expand, act2, conv3, moms.at[2])
    slide_total(2)
    home[:rows, :] = cot[me]
    for copy in cot_copies:
        copy.wait()
    result_kernel(
        m_wide, conv3, conv_short, tot.at[2], tot.at[0], gw, sw, dst, dst_t, home, up, outgoing, moms.at[3], res
    )
    out_copies = [
        send(k, outgoing.at[block(k, rows)], landed.at[me], out_send.at[k], out_recv.at[k])
        for k in range(1, peers)
    ]
    landed[me] = outgoing[:rows, :]
    slide_total(3)
    back3_kernel(
        m_wide,
        m_mid,
        up,
        conv3,
        conv_short,
        tot.at[2],
        tot.at[0],
        tot.at[3],
        gw,
        act2,
        sub_in,
        conv2,
        tot.at[1],
        gm,
        sm,
        w_expand,
        dshort,
        g_expand,
        g_short,
        back2,
        moms.at[4],
        d3,
    )
    slide_total(4)
    back2_kernel(
        m_mid,
        back2,
        conv2,
        tot.at[1],
        tot.at[4],
        gm,
        columns,
        src_t,
        w_spatial,
        ends.shape[0],
        g_spatial,
        planes,
        rim_b,
        d2,
    )
    send(peers - 1, rim_b, following, rim_send.at[1], rim_recv.at[1]).wait()
    back1_kernel(m_in, planes, following, ends, conv1, tot.at[0], gm, sm, back1, moms.at[5])
    slide_total(5)
    last_kernel(
        m_in,
        back1,
        conv1,
        tot.at[0],
        tot.at[5],
        gm,
        feat,
        w_reduce,
        dshort,
        w_short,
        sel_t,
        g_feat,
        g_reduce,
        total,
    )
    for copy in out_copies:
        copy.wait()


def share_kernel(
    groups, peers, w, vec, out, vec_out, in1, inv, mid, in2, done, in3, s1, r1, sv, rv, s2, r2, s3, r3
):
    d = lax.axis_index("dp")
    me = lax.axis_index("space")
    barrier = pltpu.get_barrier_semaphore()
    for k in range(1, groups):
        pl.semaphore_signal(
            barrier, inc=1, device_id={"dp": lax.rem(d + k, groups)}, device_id_type=MESH
        )
    for k in range(1, peers):
        pl.semaphore_signal(
            barrier, inc=1, device_id={"space": lax.rem(me + k, peers)}, device_id_type=MESH
        )
    inv[0] = vec[...]
    pl.semaphore_wait(barrier, groups + peers - 2)

    def across(k, src, dst, send, recv):
        copy = pltpu.make_async_remote_copy(
            src_ref=src,
            dst_ref=dst,
            send_sem=send.at[k],
            recv_sem=recv.at[k],
            device_id={"dp": lax.rem(d + k, groups)},
            device_id_type=MESH,
        )
        copy.start()
        return copy

    copies = []
    for k in range(1, groups):
        copies.append(across(k, w.at[lax.rem(d + k, groups)], in1.at[k], s1, r1))
        copies.append(across(k, vec, inv.at[k], sv, rv))
    for copy in copies:
        copy.wait()

    def add(i, _):
        total = w[d, i].astype(F32)
        for k in range(1, groups):
            total = total + in1[k, i].astype(F32)
        mid[i] = total.astype(BF16)
        return 0

    lax.fori_loop(0, peers, add, 0)
    copies = []
    for k in range(1, peers):
        to = lax.rem(me + k, peers)
        copy = pltpu.make_async_remote_copy(
            src_ref=mid.at[to],
            dst_ref=in2.at[k],
            send_sem=s2.at[k],
            recv_sem=r2.at[k],
            device_id={"space": to},
            device_id_type=MESH,
        )
        copy.start()
        copies.append(copy)
    total = inv[d]
    for s in range(1, groups):
        total = total + inv[lax.rem(d - s + groups, groups)]
    vec_out[...] = total
    for copy in copies:
        copy.wait()
    total = mid[me].astype(F32)
    for k in range(1, peers):
        total = total + in2[k].astype(F32)
    done[...] = total.astype(BF16)
    copies = [across(k, done, in3.at[k], s3, r3) for k in range(1, groups)]
    out[d] = done[...].astype(F32)
    for k, copy in enumerate(copies):
        copy.wait()
        out[lax.rem(d - k - 1 + groups, groups)] = in3[k + 1].astype(F32)


def share_total(w, vec):
    groups, peers = lax.axis_size("dp"), lax.axis_size("space")
    piece = w.shape[2:]
    vmem = pl.BlockSpec(memory_space=pltpu.VMEM)
    dma = pltpu.SemaphoreType.DMA
    return pl.pallas_call(
        functools.partial(share_kernel, groups, peers),
        out_shape=[
            jax.ShapeDtypeStruct((groups,) + piece, F32),
            jax.ShapeDtypeStruct(vec.shape, F32),
        ],
        in_specs=[vmem] * 2,
        out_specs=[vmem] * 2,
        scratch_shapes=[
            pltpu.VMEM(w.shape, BF16),
            pltpu.VMEM((groups,) + vec.shape, F32),
            pltpu.VMEM((peers,) + piece, BF16),
            pltpu.VMEM((peers,) + piece, BF16),
            pltpu.VMEM(piece, BF16),
            pltpu.VMEM((groups,) + piece, BF16),
            dma((groups,)),
            dma((groups,)),
            dma((groups,)),
            dma((groups,)),
            dma((peers,)),
            dma((peers,)),
            dma((groups,)),
            dma((groups,)),
        ],
        compiler_params=pltpu.CompilerParams(
            collective_id=2, has_side_effects=True, vmem_limit_bytes=24 * 1024 * 1024
        ),
    )(w, vec)


def source_rows(links, me, tiles):
    own = tiles * Q
    t = jnp.arange(tiles, dtype=jnp.int32)[:, None, None]
    i = jnp.arange(HALF, dtype=jnp.int32)[None, :, None]
    j = jnp.arange(HALF, dtype=jnp.int32)[None, None, :]
    last = HALF - 1
    far = tiles * HALF

    def away(column, r, c, along, base):
        index = links[:, column][:, None, None]
        at = index - me * tiles
        here = at * Q + r * HALF + c
        there = own + base + (at + tiles) * HALF + along
        return jnp.where(index < 0, -1, jnp.where(at >= 0, here, there))

    top = jnp.where(i > 0, t * Q + (i - 1) * HALF + j, away(0, last, j, j, 0))
    left = jnp.where(j > 0, t * Q + i * HALF + j - 1, away(1, i, last, i, 0))
    corner = jnp.where(
        i > 0,
        jnp.where(
            j > 0, t * Q + (i - 1) * HALF + j - 1, away(1, i - 1, last, i - 1, far)
        ),
        jnp.where(j > 0, away(0, last, j - 1, j - 1, 0), away(2, last, last, last, 0)),
    )
    return jnp.stack([jnp.broadcast_to(x, (tiles, HALF, HALF)).reshape(own) for x in (top, left, corner)])


def plane_order():
    order = np.zeros((STEP * SIDE * SIDE, STEP * SIDE * SIDE), np.float32)
    row = 0
    for a in range(2):
        for b in range(2):
            for t in range(STEP):
                for i in range(HALF):
                    for j in range(HALF):
                        order[row, t * SIDE * SIDE + (2 * i + a) * SIDE + 2 * j + b] = 1
                        row += 1
    return order


def rim_rows(tiles):
    ends = np.zeros((2, tiles, HALF, tiles, HALF, HALF), np.float32)
    for t in range(tiles):
        for j in range(HALF):
            ends[0, t, j, t, HALF - 1, j] = 1
            ends[1, t, j, t, j, HALF - 1] = 1
    return ends.reshape(2 * tiles * HALF, tiles * Q)


def body(
    features,
    owners,
    neighbors,
    w_reduce,
    w_spatial,
    w_expand,
    w_short,
    gm,
    sm,
    gw,
    sw,
    cotangent,
):
    spaces = lax.axis_size("space")
    groups = lax.axis_size("dp")
    me = lax.axis_index("space")
    tiles = features.shape[1]
    wide = features.shape[3]
    mid = w_reduce.shape[1]
    tiles_total = tiles * spaces
    slides = features.shape[0] * groups
    capacity = cotangent.shape[1] // spaces
    slots = spaces * capacity * Q
    own = tiles * Q
    rims = 2 * tiles * HALF
    m_in = float(tiles_total * SIDE * SIDE * (mid // GROUPS))
    m_mid = float(tiles_total * Q * (mid // GROUPS))
    m_wide = float(tiles_total * Q * (wide // GROUPS))
    order = plane_order()
    sel, sel_t = jnp.asarray(order, BF16), jnp.asarray(order.T, BF16)
    ends = jnp.asarray(rim_rows(tiles), BF16)
    src_t = source_rows(neighbors[0], me, tiles)
    src = src_t.T
    owner_of = owners[0][:, 0]
    earlier = jnp.arange(tiles)[None, :] < jnp.arange(tiles)[:, None]
    same = (owner_of[:, None] == owner_of[None, :]) & earlier
    rank_of = jnp.sum(same.astype(jnp.int32), axis=1)

    def rows_of(block_of):
        first = (lax.rem(block_of + spaces, spaces) * capacity + rank_of) * Q
        return (first[:, None] + jnp.arange(Q, dtype=jnp.int32)[None, :]).reshape(own)

    dst = rows_of(me - owner_of)[:, None]
    dst_t = rows_of(owner_of - me)[None, :]
    feat = features[0].reshape(tiles * SIDE * SIDE, wide)
    cot = cotangent[0].reshape(spaces, capacity * Q, wide)
    vmem = pl.BlockSpec(memory_space=pltpu.VMEM)
    outs = [
        ((tiles * SIDE * SIDE, wide), BF16),
        ((spaces, capacity * Q, wide), BF16),
        ((wide, mid), BF16),
        ((9 * mid, mid), BF16),
        ((mid, wide), BF16),
        ((wide, wide), BF16),
        ((6, 8, wide), F32),
    ]
    scratch = [
        ((4, own, mid), BF16),
        ((own, wide), BF16),
        ((own, wide), BF16),
        ((4, own, mid), BF16),
        ((rims, 2 * mid), BF16),
        ((rims, 2 * mid), BF16),
        ((own, 9 * mid), BF16),
        ((own, mid), BF16),
        ((own, mid), BF16),
        ((own, wide), BF16),
        ((own, wide), F32),
        ((slots, wide), BF16),
        ((own, wide), BF16),
        ((own, wide), BF16),
        ((own, mid), F32),
        ((own, wide), BF16),
        ((own, mid), BF16),
        ((4, own, mid), F32),
        ((rims, 2 * mid), BF16),
        ((rims, 2 * mid), BF16),
        ((4, own, mid), F32),
        ((wide, mid), F32),
        ((slots, wide), BF16),
        ((6, 8, wide), F32),
        ((6, spaces, 8, wide), F32),
    ]
    dma = pltpu.SemaphoreType.DMA
    semaphores = [dma((6, spaces))] * 2 + [dma((spaces,))] * 4 + [dma((2,))] * 2
    g_feat, landed, g_reduce, g_spatial, g_expand, g_short, tot = pl.pallas_call(
        functools.partial(whole_kernel, (m_in, m_mid, m_wide), spaces),
        out_shape=[jax.ShapeDtypeStruct(a, t) for a, t in outs],
        in_specs=[vmem] * 17,
        out_specs=[vmem] * len(outs),
        scratch_shapes=[pltpu.VMEM(a, t) for a, t in scratch] + semaphores,
        compiler_params=pltpu.CompilerParams(
            collective_id=1, has_side_effects=True, vmem_limit_bytes=48 * 1024 * 1024
        ),
    )(
        feat,
        cot,
        src,
        src_t,
        dst,
        dst_t,
        w_reduce,
        w_spatial,
        w_expand,
        w_short,
        gm,
        sm,
        gw,
        sw,
        sel,
        sel_t,
        ends,
    )
    block_out = landed.reshape(1, spaces * capacity, Q, wide)
    tot3b, tot2b, tot1b = tot[3], tot[4], tot[5]

    lanes = mid

    def cut(g):
        share = g.shape[0] // spaces
        wide_by = g.shape[1] // lanes
        g = g.reshape(spaces, share, wide_by, lanes).transpose(0, 2, 1, 3)
        return g.reshape(spaces, share * wide_by, lanes)

    parts = [cut(g) for g in (g_reduce, g_spatial, g_expand, g_short)]
    counts = [p.shape[1] for p in parts]
    piece = -(-sum(counts) // (groups * 16)) * 16
    filler = jnp.zeros((spaces, groups * piece - sum(counts), lanes), BF16)
    packed = jnp.concatenate(parts + [filler], axis=1)
    packed = packed.reshape(spaces, groups, piece, lanes).transpose(1, 0, 2, 3)
    vec = jnp.concatenate(
        [
            jnp.concatenate([tot1b[:2, :mid], tot2b[:2, :mid]], axis=1),
            jnp.zeros((2, wide - 2 * mid), F32),
        ],
        axis=1,
    )
    vec = jnp.concatenate([vec, tot3b[:3], jnp.zeros((3, wide), F32)], axis=0)
    shares, sums_dp = share_total(packed, vec)
    shares = shares.reshape(groups * piece, lanes)
    scale_in = 1.0 / math.sqrt(slides * tiles_total * SIDE * SIDE)
    scale_out = 1.0 / math.sqrt(slides * tiles_total * Q)

    def uncut(at, count, columns_by):
        g = shares[at : at + count].reshape(columns_by, count // columns_by, lanes)
        return g.transpose(1, 0, 2).reshape(count // columns_by, columns_by * lanes)

    def own_part(a):
        share = a.shape[1] // spaces
        return lax.dynamic_slice_in_dim(a, me * share, share, 1)

    at = [0]
    for c in counts:
        at.append(at[-1] + c)
    mid_scale = jnp.array([[scale_in], [scale_out]], F32)
    return (
        block_out,
        g_feat.reshape(1, tiles, SIDE * SIDE, wide),
        uncut(at[0], counts[0], 1) * scale_in,
        uncut(at[1], counts[1], 1) * scale_out,
        uncut(at[2], counts[2], wide // lanes) * scale_out,
        uncut(at[3], counts[3], wide // lanes) * scale_out,
        own_part(jnp.stack([sums_dp[1, :mid], sums_dp[1, mid : 2 * mid]])) * mid_scale,
        own_part(jnp.stack([sums_dp[0, :mid], sums_dp[0, mid : 2 * mid]])) * mid_scale,
        own_part(sums_dp[3:5]) * scale_out,
        own_part(jnp.stack([sums_dp[2], sums_dp[2]])) * scale_out,
    )


def solution(mesh):
    placed = (
        P("dp", "space", None, None),
        P("dp", "space", None),
        P("dp", "space", None),
        P(),
        P(),
        P(),
        P(),
        P(),
        P(),
        P(),
        P(),
        P("dp", "space", None, None),
    )
    return jax.shard_map(
        body,
        mesh=mesh,
        in_specs=placed,
        out_specs=(
            P("dp", "space", None, None),
            P("dp", "space", None, None),
            P("space", None),
            P("space", None),
            P("space", None),
            P("space", None),
            P(None, "space"),
            P(None, "space"),
            P(None, "space"),
            P(None, "space"),
        ),
        check_vma=False,
    )
```

```python
import functools
import math

import jax
import jax.numpy as jnp
import numpy as np
from jax import lax
from jax.experimental import pallas as pl
from jax.experimental.pallas import tpu as pltpu
from jax.sharding import PartitionSpec as P

GROUPS = 32
SIDE = 8
HALF = SIDE // 2
Q = HALF * HALF
EPS = 1e-05
MESH = pl.DeviceIdType.MESH
F32 = jnp.float32
BF16 = jnp.bfloat16
STEP = 4
BLOCK = 128


def sigmoid(v):
    return 1.0 / (1.0 + jnp.exp(-v))


def smooth(v):
    return v * sigmoid(v)


def slope(v):
    s = sigmoid(v)
    return s * (1.0 + v * (1.0 - s))


def mm(a, b):
    return lax.dot_general(a, b, (((1,), (0,)), ((), ())), preferred_element_type=F32)


def mm_t(a, b):
    return lax.dot_general(a, b, (((1,), (1,)), ((), ())), preferred_element_type=F32)


def t_mm(a, b):
    return lax.dot_general(a, b, (((0,), (0,)), ((), ())), preferred_element_type=F32)


def group_sum(rows):
    width = rows.shape[-1]
    each = width // GROUPS
    a = lax.broadcasted_iota(jnp.int32, (width, width), 0) // each
    b = lax.broadcasted_iota(jnp.int32, (width, width), 1) // each
    same = jnp.where(a == b, 1.0, 0.0).astype(F32)
    return lax.dot_general(
        rows,
        same,
        (((1,), (0,)), ((), ())),
        precision=lax.Precision.HIGHEST,
        preferred_element_type=F32,
    )


def norm_of(tot, first, width, members):
    g = group_sum(tot[:, :width])
    center = g[first : first + 1] / members
    spread = g[first + 1 : first + 2] / members - center * center
    return center, lax.rsqrt(spread + EPS)


def back_of(tot, first, second, gain, width, members):
    g = group_sum(tot[:, :width] * gain)
    return g[first : first + 1] / members, g[second : second + 1] / members


def sums(v):
    return jnp.sum(v, axis=0, keepdims=True)


def onehot(index, axis, shape):
    return jnp.where(lax.broadcasted_iota(jnp.int32, shape, axis) == index, 1.0, 0.0).astype(BF16)


def block(i, size):
    start = i * size
    return pl.ds(start if isinstance(start, int) else pl.multiple_of(start, size), size)


def first_kernel(feat, w_reduce, w_short, sel, conv1, sub_in, conv_short, mom):
    rows = STEP * SIDE * SIDE
    part = STEP * Q
    wide = w_short.shape[1]
    mid = w_reduce.shape[1]

    def step(g, carry):
        s1, q1, s2, q2 = carry
        x = feat[block(g, rows), :]
        c = mm(x, w_reduce[...]).astype(BF16)
        cf = c.astype(F32)
        p = mm(sel[...], c).astype(BF16)
        for k in range(4):
            conv1[k, block(g, part), :] = p[k * part : (k + 1) * part]
        sub = mm(sel[:part, :], x).astype(BF16)
        sub_in[block(g, part), :] = sub
        sh = mm(sub, w_short[...]).astype(BF16)
        conv_short[block(g, part), :] = sh
        sf = sh.astype(F32)
        return s1 + sums(cf), q1 + sums(cf * cf), s2 + sums(sf), q2 + sums(sf * sf)

    z1, z2 = jnp.zeros((1, mid), F32), jnp.zeros((1, wide), F32)
    s1, q1, s2, q2 = lax.fori_loop(0, feat.shape[0] // rows, step, (z1, z1, z2, z2))
    mom[...] = jnp.zeros_like(mom)
    mom[0:1, :mid] = s1
    mom[1:2, :mid] = q1
    mom[2:3, :] = s2
    mom[3:4, :] = q2


def act_kernel(members, conv1, tot1, gm, sm, ends, act, rim):
    mid = conv1.shape[2]
    center, inv = norm_of(tot1[...], 0, mid, members)
    for k in range(4):

        def step(i, _, k=k):
            v = (conv1[k, block(i, BLOCK), :].astype(F32) - center) * inv
            act[k, block(i, BLOCK), :] = smooth(v * gm[0:1] + sm[0:1]).astype(BF16)
            return 0

        lax.fori_loop(0, conv1.shape[1] // BLOCK, step, 0)
    count = ends.shape[0] // 2
    for k, e, lane in ((2, 0, 0), (3, 0, 1), (1, 1, 0), (3, 1, 1)):
        rim[e * count : (e + 1) * count, lane * mid : (lane + 1) * mid] = mm(
            ends[e * count : (e + 1) * count, :], act[k]
        ).astype(BF16)


def conv2_kernel(act, rim, src, w_spatial, columns, conv2, mom):
    mid = act.shape[2]
    own = act.shape[1]
    far = rim.shape[0] // 2

    def step(i, carry):
        s, q = carry
        rows = block(i, BLOCK)
        at = src[rows, :]
        top = onehot(at[:, 0:1], 1, (BLOCK, own + far))
        left = onehot(at[:, 1:2], 1, (BLOCK, own + far))
        corner = onehot(at[:, 2:3], 1, (BLOCK, own + 2 * far))

        def put(slot, v):
            columns[rows, slot * mid : (slot + 1) * mid] = v.astype(BF16)

        put(1, mm(top[:, :own], act[2]) + mm(top[:, own:], rim[:far, :mid]))
        put(2, mm(top[:, :own], act[3]) + mm(top[:, own:], rim[:far, mid:]))
        put(3, mm(left[:, :own], act[1]) + mm(left[:, own:], rim[far:, :mid]))
        put(6, mm(left[:, :own], act[3]) + mm(left[:, own:], rim[far:, mid:]))
        put(0, mm(corner[:, :own], act[3]) + mm(corner[:, own:], rim[:, mid:]))
        for slot, k in ((4, 0), (5, 1), (7, 2), (8, 3)):
            columns[rows, slot * mid : (slot + 1) * mid] = act[k, rows, :]
        c = mm(columns[rows, :], w_spatial[...]).astype(BF16)
        conv2[rows, :] = c
        cf = c.astype(F32)
        return s + sums(cf), q + sums(cf * cf)

    z = jnp.zeros((1, mid), F32)
    s, q = lax.fori_loop(0, own // BLOCK, step, (z, z))
    mom[...] = jnp.zeros_like(mom)
    mom[0:1, :mid] = s
    mom[1:2, :mid] = q


def conv3_kernel(members, conv2, tot2, gm, sm, w_expand, act2, conv3, mom):
    mid = conv2.shape[1]
    center, inv = norm_of(tot2[...], 0, mid, members)

    def step(i, carry):
        s, q = carry
        rows = block(i, BLOCK)
        v = (conv2[rows, :].astype(F32) - center) * inv
        a = smooth(v * gm[1:2] + sm[1:2]).astype(BF16)
        act2[rows, :] = a
        c = mm(a, w_expand[...]).astype(BF16)
        conv3[rows, :] = c
        cf = c.astype(F32)
        return s + sums(cf), q + sums(cf * cf)

    z = jnp.zeros((1, conv3.shape[1]), F32)
    s, q = lax.fori_loop(0, conv2.shape[0] // BLOCK, step, (z, z))
    mom[...] = jnp.zeros_like(mom)
    mom[0:1, :] = s
    mom[1:2, :] = q


def result_kernel(
    members, conv3, conv_short, tot3, tot1, gw, sw, dst, dst_t, cot, up, outgoing, mom, res
):
    wide = conv3.shape[1]
    rows_all = conv3.shape[0]
    slots = cot.shape[0]
    c3, i3 = norm_of(tot3[...], 0, wide, members)
    cs, is_ = norm_of(tot1[...], 2, wide, members)

    def step(i, carry):
        a, b, c = carry
        rows = block(i, BLOCK)
        n3 = (conv3[rows, :].astype(F32) - c3) * i3
        ns = (conv_short[rows, :].astype(F32) - cs) * is_
        summed = n3 * gw[0:1] + sw[0:1] + (ns * gw[1:2] + sw[1:2])
        res[rows, :] = smooth(summed).astype(BF16)
        picked = mm(onehot(dst[rows, :], 1, (BLOCK, slots)), cot[...])
        u = picked * slope(summed)
        up[rows, :] = u
        return a + sums(u), b + sums(u * n3), c + sums(u * ns)

    z = jnp.zeros((1, wide), F32)
    a, b, c = lax.fori_loop(0, rows_all // BLOCK, step, (z, z, z))
    mom[...] = jnp.zeros_like(mom)
    mom[0:1, :] = a
    mom[1:2, :] = b
    mom[2:3, :] = c

    def send(i, _):
        at = dst_t[...] - i * BLOCK
        outgoing[block(i, BLOCK), :] = mm(onehot(at, 0, (BLOCK, rows_all)), res[...]).astype(BF16)
        return 0

    lax.fori_loop(0, slots // BLOCK, send, 0)


def back3_kernel(
    wide_members,
    mid_members,
    up,
    conv3,
    conv_short,
    tot3,
    tot1,
    totb,
    gw,
    act2,
    sub_in,
    conv2,
    tot2,
    gm,
    sm,
    w_expand,
    dshort,
    g_expand,
    g_short,
    back2,
    mom,
    d3,
):
    wide = conv3.shape[1]
    mid = conv2.shape[1]
    rows_all = conv3.shape[0]
    c3, i3 = norm_of(tot3[...], 0, wide, wide_members)
    cs, is_ = norm_of(tot1[...], 2, wide, wide_members)
    f3, h3 = back_of(totb[...], 0, 1, gw[0:1], wide, wide_members)
    fs, hs = back_of(totb[...], 0, 2, gw[1:2], wide, wide_members)
    c2, i2 = norm_of(tot2[...], 0, mid, mid_members)

    def step(i, carry):
        s, q = carry
        rows = block(i, BLOCK)
        u = up[rows, :]
        n3 = (conv3[rows, :].astype(F32) - c3) * i3
        ns = (conv_short[rows, :].astype(F32) - cs) * is_
        d = (i3 * (gw[0:1] * u - f3 - n3 * h3)).astype(BF16)
        d3[rows, :] = d
        dshort[rows, :] = (is_ * (gw[1:2] * u - fs - ns * hs)).astype(BF16)
        n2 = (conv2[rows, :].astype(F32) - c2) * i2
        b = mm_t(d, w_expand[...]) * slope(n2 * gm[1:2] + sm[1:2])
        back2[rows, :] = b
        return s + sums(b), q + sums(b * n2)

    z = jnp.zeros((1, mid), F32)
    s, q = lax.fori_loop(0, rows_all // BLOCK, step, (z, z))
    mom[...] = jnp.zeros_like(mom)
    mom[0:1, :mid] = s
    mom[1:2, :mid] = q
    g_expand[...] = t_mm(act2[...], d3[...]).astype(BF16)

    for j in range(wide // BLOCK):
        cut = slice(j * BLOCK, (j + 1) * BLOCK)
        g_short[cut, :] = t_mm(sub_in[:, cut], dshort[...]).astype(BF16)


def back2_kernel(
    members,
    back2,
    conv2,
    tot2,
    totb,
    gm,
    columns,
    src_t,
    w_spatial,
    rims,
    g_spatial,
    planes,
    rim,
    d2,
):
    mid = conv2.shape[1]
    own = conv2.shape[0]
    far = rims // 2
    c2, i2 = norm_of(tot2[...], 0, mid, members)
    f2, h2 = back_of(totb[...], 0, 1, gm[1:2], mid, members)
    n2 = (conv2[...].astype(F32) - c2) * i2
    d2[...] = (i2 * (gm[1:2] * back2[...] - f2 - n2 * h2)).astype(BF16)
    d = d2[...]

    def part(slot):
        return mm_t(d, w_spatial[slot * mid : (slot + 1) * mid, :])

    for slot in range(9):
        cut = slice(slot * mid, (slot + 1) * mid)
        g_spatial[cut, :] = t_mm(columns[:, cut], d).astype(BF16)
    top_a, top_b = part(1).astype(BF16), part(2).astype(BF16)
    left_a, left_b = part(3).astype(BF16), part(6).astype(BF16)
    corner = part(0).astype(BF16)
    planes[0] = part(4)
    planes[1] = part(5)
    planes[2] = part(7)
    planes[3] = part(8)
    top_at, left_at, corner_at = src_t[0:1, :], src_t[1:2, :], src_t[2:3, :]

    def step(i, _):
        rows = block(i, BLOCK)
        top = onehot(top_at - i * BLOCK, 0, (BLOCK, own))
        left = onehot(left_at - i * BLOCK, 0, (BLOCK, own))
        both = onehot(corner_at - i * BLOCK, 0, (BLOCK, own))
        planes[1, rows, :] += mm(left, left_a)
        planes[2, rows, :] += mm(top, top_a)
        planes[3, rows, :] += mm(top, top_b) + mm(left, left_b) + mm(both, corner)
        return 0

    lax.fori_loop(0, own // BLOCK, step, 0)
    top = onehot(top_at - own, 0, (far, own))
    left = onehot(left_at - own, 0, (far, own))
    over = onehot(corner_at - own, 0, (far, own))
    beside = onehot(corner_at - own - far, 0, (far, own))
    rim[:far, :mid] = mm(top, top_a).astype(BF16)
    rim[:far, mid:] = (mm(top, top_b) + mm(over, corner)).astype(BF16)
    rim[far:, :mid] = mm(left, left_a).astype(BF16)
    rim[far:, mid:] = (mm(left, left_b) + mm(beside, corner)).astype(BF16)


def back1_kernel(members, planes, rim, ends, conv1, tot1, gm, sm, back1, mom):
    mid = conv1.shape[2]
    far = ends.shape[0] // 2
    center, inv = norm_of(tot1[...], 0, mid, members)
    s = q = jnp.zeros((1, mid), F32)
    for k in range(4):
        v = planes[k]
        if k >= 2:
            v = v + t_mm(ends[:far, :], rim[:far, (k - 2) * mid : (k - 1) * mid])
        if k % 2:
            lane = k // 2
            v = v + t_mm(ends[far:, :], rim[far:, lane * mid : (lane + 1) * mid])
        n = (conv1[k].astype(F32) - center) * inv
        b = v * slope(n * gm[0:1] + sm[0:1])
        back1[k] = b
        s, q = s + sums(b), q + sums(b * n)
    mom[...] = jnp.zeros_like(mom)
    mom[0:1, :mid] = s
    mom[1:2, :mid] = q


def last_kernel(
    members,
    back1,
    conv1,
    tot1,
    totb,
    gm,
    feat,
    w_reduce,
    dshort,
    w_short,
    sel_t,
    g_feat,
    g_reduce,
    total,
):
    mid = conv1.shape[2]
    rows = STEP * SIDE * SIDE
    part = STEP * Q
    center, inv = norm_of(tot1[...], 0, mid, members)
    first, second = back_of(totb[...], 0, 1, gm[0:1], mid, members)
    total[...] = jnp.zeros_like(total)

    def step(g, _):
        cuts = []
        for k in range(4):
            n = (conv1[k, block(g, part), :].astype(F32) - center) * inv
            u = back1[k, block(g, part), :]
            cuts.append((inv * (gm[0:1] * u - first - n * second)).astype(BF16))
        d = jnp.concatenate(cuts, axis=0)
        total[...] += t_mm(feat[block(g, rows), :], mm(sel_t[...], d).astype(BF16))
        short = mm_t(dshort[block(g, part), :], w_short[...])
        back = mm_t(d, w_reduce[...])
        back = jnp.concatenate([back[:part] + short, back[part:]], axis=0).astype(BF16)
        g_feat[block(g, rows), :] = mm(sel_t[...], back).astype(BF16)
        return 0

    lax.fori_loop(0, feat.shape[0] // rows, step, 0)
    g_reduce[...] = total[...].astype(BF16)


def whole_kernel(members, peers, *refs):
    m_in, m_mid, m_wide = members
    (feat_in, cot, src, src_t, dst, dst_t, w_reduce, w_spatial, w_expand, w_short, gm, sm, gw, sw) = refs[:14]
    sel, sel_t, ends = refs[14:17]
    g_feat, landed, g_reduce, g_spatial, g_expand, g_short, tot = refs[17:24]
    (conv1, sub_in, conv_short, act, rim, prior, columns, conv2, act2, conv3) = refs[24:34]
    (up, outgoing, res, dshort, back2, d3, d2, planes, rim_b, following, back1) = refs[34:45]
    total, home, moms, slots, feat = refs[45:50]
    sum_send, sum_recv, cot_send, cot_recv, out_send, out_recv, rim_send, rim_recv, own_sem = refs[50:]
    me = lax.axis_index("space")
    rows = cot.shape[1]
    mid = conv2.shape[1]
    feat_copy = pltpu.make_async_copy(feat_in, feat, own_sem.at[0])
    feat_copy.start()
    cot_copy = pltpu.make_async_copy(cot.at[me], home.at[:rows], own_sem.at[1])
    cot_copy.start()
    barrier = pltpu.get_barrier_semaphore()
    for k in range(1, peers):
        pl.semaphore_signal(
            barrier, inc=1, device_id={"space": lax.rem(me + k, peers)}, device_id_type=MESH
        )
    pl.semaphore_wait(barrier, peers - 1)

    def send(by, source, target, out_sem, in_sem):
        copy = pltpu.make_async_remote_copy(
            src_ref=source,
            dst_ref=target,
            send_sem=out_sem,
            recv_sem=in_sem,
            device_id={"space": lax.rem(me + by, peers)},
            device_id_type=MESH,
        )
        copy.start()
        return copy

    def slide_total(n, width):
        copies = [
            send(
                k,
                moms.at[n, :, :width],
                slots.at[n, k, :, :width],
                sum_send.at[n, k],
                sum_recv.at[n, k],
            )
            for k in range(1, peers)
        ]
        slots[n, 0, :, :width] = moms[n, :, :width]
        for copy in copies:
            copy.wait()
        sum_of = slots[n, me, :, :width]
        for s in range(1, peers):
            sum_of = sum_of + slots[n, lax.rem(me - s + peers, peers), :, :width]
        tot[n, :, :width] = sum_of

    cot_copies, out_copies = [], []

    def send_cot(first, last):
        for k in range(1 + (peers - 1) * first // 7, 1 + (peers - 1) * last // 7):
            to = lax.rem(me + k, peers)
            cot_copies.append(
                send(k, cot.at[to], home.at[block(k, rows)], cot_send.at[k], cot_recv.at[k])
            )

    def send_out(first, last):
        for k in range(1 + (peers - 1) * first // 7, 1 + (peers - 1) * last // 7):
            out_copies.append(
                send(k, outgoing.at[block(k, rows)], landed.at[me], out_send.at[k], out_recv.at[k])
            )

    wide = conv3.shape[1]
    tot[...] = jnp.zeros_like(tot)
    send_cot(0, 2)
    feat_copy.wait()
    first_kernel(feat, w_reduce, w_short, sel, conv1, sub_in, conv_short, moms.at[0])
    slide_total(0, mid)
    send_cot(2, 3)
    act_kernel(m_in, conv1, tot.at[0], gm, sm, ends, act, rim)
    send(1, rim, prior, rim_send.at[0], rim_recv.at[0]).wait()
    send_cot(3, 4)
    conv2_kernel(act, prior, src, w_spatial, columns, conv2, moms.at[1])
    slide_total(1, mid)
    send_cot(4, 5)
    conv3_kernel(m_mid, conv2, tot.at[1], gm, sm, w_expand, act2, conv3, moms.at[2])
    moms[2, 2:4, :] = moms[0, 2:4, :]
    send_cot(5, 7)
    slide_total(2, wide)
    cot_copy.wait()
    for copy in cot_copies:
        copy.wait()
    result_kernel(
        m_wide, conv3, conv_short, tot.at[2], tot.at[2], gw, sw, dst, dst_t, home, up, outgoing, moms.at[3], res
    )
    landed[me] = outgoing[:rows, :]
    slide_total(3, wide)
    send_out(0, 1)
    back3_kernel(
        m_wide,
        m_mid,
        up,
        conv3,
        conv_short,
        tot.at[2],
        tot.at[2],
        tot.at[3],
        gw,
        act2,
        sub_in,
        conv2,
        tot.at[1],
        gm,
        sm,
        w_expand,
        dshort,
        g_expand,
        g_short,
        back2,
        moms.at[4],
        d3,
    )
    slide_total(4, mid)
    send_out(1, 2)
    back2_kernel(
        m_mid,
        back2,
        conv2,
        tot.at[1],
        tot.at[4],
        gm,
        columns,
        src_t,
        w_spatial,
        ends.shape[0],
        g_spatial,
        planes,
        rim_b,
        d2,
    )
    send(peers - 1, rim_b, following, rim_send.at[1], rim_recv.at[1]).wait()
    back1_kernel(m_in, planes, following, ends, conv1, tot.at[0], gm, sm, back1, moms.at[5])
    slide_total(5, mid)
    send_out(2, 7)
    last_kernel(
        m_in,
        back1,
        conv1,
        tot.at[0],
        tot.at[5],
        gm,
        feat,
        w_reduce,
        dshort,
        w_short,
        sel_t,
        g_feat,
        g_reduce,
        total,
    )
    for copy in out_copies:
        copy.wait()


def share_kernel(
    groups, peers, w, vec, out, vec_out, in1, inv, mid, in2, done, in3, s1, r1, sv, rv, s2, r2, s3, r3
):
    d = lax.axis_index("dp")
    me = lax.axis_index("space")
    barrier = pltpu.get_barrier_semaphore()
    for k in range(1, groups):
        pl.semaphore_signal(
            barrier, inc=1, device_id={"dp": lax.rem(d + k, groups)}, device_id_type=MESH
        )
    for k in range(1, peers):
        pl.semaphore_signal(
            barrier, inc=1, device_id={"space": lax.rem(me + k, peers)}, device_id_type=MESH
        )
    inv[0] = vec[...]
    pl.semaphore_wait(barrier, groups + peers - 2)

    def across(k, src, dst, send, recv):
        copy = pltpu.make_async_remote_copy(
            src_ref=src,
            dst_ref=dst,
            send_sem=send.at[k],
            recv_sem=recv.at[k],
            device_id={"dp": lax.rem(d + k, groups)},
            device_id_type=MESH,
        )
        copy.start()
        return copy

    copies = []
    for k in range(1, groups):
        copies.append(across(k, w.at[lax.rem(d + k, groups)], in1.at[k], s1, r1))
        copies.append(across(k, vec, inv.at[k], sv, rv))
    for copy in copies:
        copy.wait()

    def add(i, _):
        total = w[d, i].astype(F32)
        for k in range(1, groups):
            total = total + in1[k, i].astype(F32)
        mid[i] = total.astype(BF16)
        return 0

    lax.fori_loop(0, peers, add, 0)
    copies = []
    for k in range(1, peers):
        to = lax.rem(me + k, peers)
        copy = pltpu.make_async_remote_copy(
            src_ref=mid.at[to],
            dst_ref=in2.at[k],
            send_sem=s2.at[k],
            recv_sem=r2.at[k],
            device_id={"space": to},
            device_id_type=MESH,
        )
        copy.start()
        copies.append(copy)
    total = inv[d]
    for s in range(1, groups):
        total = total + inv[lax.rem(d - s + groups, groups)]
    vec_out[...] = total
    for copy in copies:
        copy.wait()
    total = mid[me].astype(F32)
    for k in range(1, peers):
        total = total + in2[k].astype(F32)
    done[...] = total.astype(BF16)
    copies = [across(k, done, in3.at[k], s3, r3) for k in range(1, groups)]
    out[d] = done[...].astype(F32)
    for k, copy in enumerate(copies):
        copy.wait()
        out[lax.rem(d - k - 1 + groups, groups)] = in3[k + 1].astype(F32)


def share_total(w, vec):
    groups, peers = lax.axis_size("dp"), lax.axis_size("space")
    piece = w.shape[2:]
    vmem = pl.BlockSpec(memory_space=pltpu.VMEM)
    dma = pltpu.SemaphoreType.DMA
    return pl.pallas_call(
        functools.partial(share_kernel, groups, peers),
        out_shape=[
            jax.ShapeDtypeStruct((groups,) + piece, F32),
            jax.ShapeDtypeStruct(vec.shape, F32),
        ],
        in_specs=[vmem] * 2,
        out_specs=[vmem] * 2,
        scratch_shapes=[
            pltpu.VMEM(w.shape, BF16),
            pltpu.VMEM((groups,) + vec.shape, F32),
            pltpu.VMEM((peers,) + piece, BF16),
            pltpu.VMEM((peers,) + piece, BF16),
            pltpu.VMEM(piece, BF16),
            pltpu.VMEM((groups,) + piece, BF16),
            dma((groups,)),
            dma((groups,)),
            dma((groups,)),
            dma((groups,)),
            dma((peers,)),
            dma((peers,)),
            dma((groups,)),
            dma((groups,)),
        ],
        compiler_params=pltpu.CompilerParams(
            collective_id=2, has_side_effects=True, vmem_limit_bytes=24 * 1024 * 1024
        ),
    )(w, vec)


def source_rows(links, me, tiles):
    own = tiles * Q
    t = jnp.arange(tiles, dtype=jnp.int32)[:, None, None]
    i = jnp.arange(HALF, dtype=jnp.int32)[None, :, None]
    j = jnp.arange(HALF, dtype=jnp.int32)[None, None, :]
    last = HALF - 1
    far = tiles * HALF

    def away(column, r, c, along, base):
        index = links[:, column][:, None, None]
        at = index - me * tiles
        here = at * Q + r * HALF + c
        there = own + base + (at + tiles) * HALF + along
        return jnp.where(index < 0, -1, jnp.where(at >= 0, here, there))

    top = jnp.where(i > 0, t * Q + (i - 1) * HALF + j, away(0, last, j, j, 0))
    left = jnp.where(j > 0, t * Q + i * HALF + j - 1, away(1, i, last, i, 0))
    corner = jnp.where(
        i > 0,
        jnp.where(
            j > 0, t * Q + (i - 1) * HALF + j - 1, away(1, i - 1, last, i - 1, far)
        ),
        jnp.where(j > 0, away(0, last, j - 1, j - 1, 0), away(2, last, last, last, 0)),
    )
    return jnp.stack([jnp.broadcast_to(x, (tiles, HALF, HALF)).reshape(own) for x in (top, left, corner)])


def plane_order():
    order = np.zeros((STEP * SIDE * SIDE, STEP * SIDE * SIDE), np.float32)
    row = 0
    for a in range(2):
        for b in range(2):
            for t in range(STEP):
                for i in range(HALF):
                    for j in range(HALF):
                        order[row, t * SIDE * SIDE + (2 * i + a) * SIDE + 2 * j + b] = 1
                        row += 1
    return order


def rim_rows(tiles):
    ends = np.zeros((2, tiles, HALF, tiles, HALF, HALF), np.float32)
    for t in range(tiles):
        for j in range(HALF):
            ends[0, t, j, t, HALF - 1, j] = 1
            ends[1, t, j, t, j, HALF - 1] = 1
    return ends.reshape(2 * tiles * HALF, tiles * Q)


def body(
    features,
    owners,
    neighbors,
    w_reduce,
    w_spatial,
    w_expand,
    w_short,
    gm,
    sm,
    gw,
    sw,
    cotangent,
):
    spaces = lax.axis_size("space")
    groups = lax.axis_size("dp")
    me = lax.axis_index("space")
    tiles = features.shape[1]
    wide = features.shape[3]
    mid = w_reduce.shape[1]
    tiles_total = tiles * spaces
    slides = features.shape[0] * groups
    capacity = cotangent.shape[1] // spaces
    slots = spaces * capacity * Q
    own = tiles * Q
    rims = 2 * tiles * HALF
    m_in = float(tiles_total * SIDE * SIDE * (mid // GROUPS))
    m_mid = float(tiles_total * Q * (mid // GROUPS))
    m_wide = float(tiles_total * Q * (wide // GROUPS))
    order = plane_order()
    sel, sel_t = jnp.asarray(order, BF16), jnp.asarray(order.T, BF16)
    ends = jnp.asarray(rim_rows(tiles), BF16)
    src_t = source_rows(neighbors[0], me, tiles)
    src = src_t.T
    owner_of = owners[0][:, 0]
    earlier = jnp.arange(tiles)[None, :] < jnp.arange(tiles)[:, None]
    same = (owner_of[:, None] == owner_of[None, :]) & earlier
    rank_of = jnp.sum(same.astype(jnp.int32), axis=1)

    def rows_of(block_of):
        first = (lax.rem(block_of + spaces, spaces) * capacity + rank_of) * Q
        return (first[:, None] + jnp.arange(Q, dtype=jnp.int32)[None, :]).reshape(own)

    dst = rows_of(me - owner_of)[:, None]
    dst_t = rows_of(owner_of - me)[None, :]
    feat = features[0].reshape(tiles * SIDE * SIDE, wide)
    cot = cotangent[0].reshape(spaces, capacity * Q, wide)
    vmem = pl.BlockSpec(memory_space=pltpu.VMEM)
    outs = [
        ((tiles * SIDE * SIDE, wide), BF16),
        ((spaces, capacity * Q, wide), BF16),
        ((wide, mid), BF16),
        ((9 * mid, mid), BF16),
        ((mid, wide), BF16),
        ((wide, wide), BF16),
        ((6, 8, wide), F32),
    ]
    scratch = [
        ((4, own, mid), BF16),
        ((own, wide), BF16),
        ((own, wide), BF16),
        ((4, own, mid), BF16),
        ((rims, 2 * mid), BF16),
        ((rims, 2 * mid), BF16),
        ((own, 9 * mid), BF16),
        ((own, mid), BF16),
        ((own, mid), BF16),
        ((own, wide), BF16),
        ((own, wide), F32),
        ((slots, wide), BF16),
        ((own, wide), BF16),
        ((own, wide), BF16),
        ((own, mid), F32),
        ((own, wide), BF16),
        ((own, mid), BF16),
        ((4, own, mid), F32),
        ((rims, 2 * mid), BF16),
        ((rims, 2 * mid), BF16),
        ((4, own, mid), F32),
        ((wide, mid), F32),
        ((slots, wide), BF16),
        ((6, 8, wide), F32),
        ((6, spaces, 8, wide), F32),
        (feat.shape, BF16),
    ]
    dma = pltpu.SemaphoreType.DMA
    semaphores = [dma((6, spaces))] * 2 + [dma((spaces,))] * 4 + [dma((2,))] * 3
    g_feat, landed, g_reduce, g_spatial, g_expand, g_short, tot = pl.pallas_call(
        functools.partial(whole_kernel, (m_in, m_mid, m_wide), spaces),
        out_shape=[jax.ShapeDtypeStruct(a, t) for a, t in outs],
        in_specs=[pl.BlockSpec(memory_space=pl.ANY)] * 2 + [vmem] * 15,
        out_specs=[vmem] * len(outs),
        scratch_shapes=[pltpu.VMEM(a, t) for a, t in scratch] + semaphores,
        compiler_params=pltpu.CompilerParams(
            collective_id=1, has_side_effects=True, vmem_limit_bytes=48 * 1024 * 1024
        ),
    )(
        feat,
        cot,
        src,
        src_t,
        dst,
        dst_t,
        w_reduce,
        w_spatial,
        w_expand,
        w_short,
        gm,
        sm,
        gw,
        sw,
        sel,
        sel_t,
        ends,
    )
    block_out = landed.reshape(1, spaces * capacity, Q, wide)
    tot3b, tot2b, tot1b = tot[3], tot[4], tot[5]

    lanes = mid

    def cut(g):
        share = g.shape[0] // spaces
        wide_by = g.shape[1] // lanes
        g = g.reshape(spaces, share, wide_by, lanes).transpose(0, 2, 1, 3)
        return g.reshape(spaces, share * wide_by, lanes)

    parts = [cut(g) for g in (g_reduce, g_spatial, g_expand, g_short)]
    counts = [p.shape[1] for p in parts]
    piece = -(-sum(counts) // (groups * 16)) * 16
    filler = jnp.zeros((spaces, groups * piece - sum(counts), lanes), BF16)
    packed = jnp.concatenate(parts + [filler], axis=1)
    packed = packed.reshape(spaces, groups, piece, lanes).transpose(1, 0, 2, 3)
    vec = jnp.concatenate(
        [
            jnp.concatenate([tot1b[:2, :mid], tot2b[:2, :mid]], axis=1),
            jnp.zeros((2, wide - 2 * mid), F32),
        ],
        axis=1,
    )
    vec = jnp.concatenate([vec, tot3b[:3], jnp.zeros((3, wide), F32)], axis=0)
    shares, sums_dp = share_total(packed, vec)
    shares = shares.reshape(groups * piece, lanes)
    scale_in = 1.0 / math.sqrt(slides * tiles_total * SIDE * SIDE)
    scale_out = 1.0 / math.sqrt(slides * tiles_total * Q)

    def uncut(at, count, columns_by):
        g = shares[at : at + count].reshape(columns_by, count // columns_by, lanes)
        return g.transpose(1, 0, 2).reshape(count // columns_by, columns_by * lanes)

    def own_part(a):
        share = a.shape[1] // spaces
        return lax.dynamic_slice_in_dim(a, me * share, share, 1)

    at = [0]
    for c in counts:
        at.append(at[-1] + c)
    mid_scale = jnp.array([[scale_in], [scale_out]], F32)
    return (
        block_out,
        g_feat.reshape(1, tiles, SIDE * SIDE, wide),
        uncut(at[0], counts[0], 1) * scale_in,
        uncut(at[1], counts[1], 1) * scale_out,
        uncut(at[2], counts[2], wide // lanes) * scale_out,
        uncut(at[3], counts[3], wide // lanes) * scale_out,
        own_part(jnp.stack([sums_dp[1, :mid], sums_dp[1, mid : 2 * mid]])) * mid_scale,
        own_part(jnp.stack([sums_dp[0, :mid], sums_dp[0, mid : 2 * mid]])) * mid_scale,
        own_part(sums_dp[3:5]) * scale_out,
        own_part(jnp.stack([sums_dp[2], sums_dp[2]])) * scale_out,
    )


def solution(mesh):
    placed = (
        P("dp", "space", None, None),
        P("dp", "space", None),
        P("dp", "space", None),
        P(),
        P(),
        P(),
        P(),
        P(),
        P(),
        P(),
        P(),
        P("dp", "space", None, None),
    )
    return jax.shard_map(
        body,
        mesh=mesh,
        in_specs=placed,
        out_specs=(
            P("dp", "space", None, None),
            P("dp", "space", None, None),
            P("space", None),
            P("space", None),
            P("space", None),
            P("space", None),
            P(None, "space"),
            P(None, "space"),
            P(None, "space"),
            P(None, "space"),
        ),
        check_vma=False,
    )
```
